128 devices in a mesh: dp: 8 (over y, core), mp: 16 (over z, x).
Axes of the slice: x: 4, y: 4, z: 4, core: 2. Of those that a mesh axis runs over, the one named last changes fastest.
Arguments:
- saved_acts: bfloat16 [6144, 18432], P('dp', 'mp'), may hold values from -6 to 6
- solution: float32 [18432, 4608], P('mp', 'dp'), may hold values from -6 to 6
- residual: float32 [18432, 4608], P('mp', 'dp'), may hold values from -6 to 6
- direction: float32 [18432, 4608], P('mp', 'dp'), may hold values from -6 to 6
Outputs:
- new_solution: float32 [18432, 4608], P('mp', 'dp')
- new_residual: float32 [18432, 4608], P('mp', 'dp')
- new_direction: float32 [18432, 4608], P('mp', 'dp')
The draws below stay inside these ranges and needn't reach their ends.
All inputs are finite; a program needn't handle non-finite values.
Results may differ from the reference program's by a relative error of at most 0.0029.
Values may be sent and summed in bfloat16 or wider, within the bound.
A program may use at most 128 MiB of HBM per device.

```python
import jax
import jax.numpy as jnp
from jax import lax

D = 4608
FF = 18432
TOKENS = 6144


def block_levels(rng, extent, pieces, smallest, top_value):
    gain, own = 1.0, jax.random.fold_in(rng, 6)
    for axis_at, shards_of in pieces:
        heights = jnp.exp(jax.random.uniform(jax.random.fold_in(own, axis_at), (shards_of,), jnp.float32, smallest / len(pieces), top_value / len(pieces)))
        gain = gain * jnp.repeat(heights, extent[axis_at] // shards_of).reshape([-1 if axis == axis_at else 1 for axis in range(len(extent))])
    return gain


def normal_values(stream_key, shape, spread, limit, cuts=(), held_as=jnp.bfloat16):
    values = jax.random.normal(stream_key, shape, jnp.float32) * spread
    if len(cuts) > 0:
        values = block_levels(stream_key, shape, cuts, -0.22, 0.18) * values
    return jnp.clip(values, min=-limit, max=limit).astype(held_as)


def setup_inputs(seed: int = 0) -> dict:
    seeds = jax.random.split(jax.random.key(seed), 5)
    saved_acts = normal_values(seeds[0], (TOKENS, FF), 1.0, 6.0, ((0, 8), (1, 16)))
    solution = normal_values(seeds[1], (FF, D), 1.0, 6.0, ((0, 16), (1, 8)), jnp.float32)
    residual = normal_values(seeds[2], (FF, D), 1.0, 6.0, ((0, 16), (1, 8)), jnp.float32)
    direction = normal_values(seeds[3], (FF, D), 1.0, 6.0, ((0, 16), (1, 8)), jnp.float32)
    return {"saved_acts": saved_acts, "solution": solution, "residual": residual, "direction": direction}


def reference(saved_acts, solution, residual, direction):
    low_dir = direction.astype(jnp.bfloat16)
    tangent = jnp.dot(saved_acts, low_dir, preferred_element_type=jnp.float32).astype(jnp.bfloat16)
    pulled = lax.dot_general(saved_acts, tangent, (((0,), (0,)), ((), ())), preferred_element_type=jnp.float32)
    curved = pulled / TOKENS + 1.0 * direction
    norm_old = jnp.sum(residual * residual)
    along = jnp.sum(direction * curved)
    step_size = norm_old / along
    new_solution = solution + step_size * direction
    new_residual = residual - step_size * curved
    norm_new = jnp.sum(new_residual * new_residual)
    new_direction = new_residual + (norm_new / norm_old) * direction
    return new_solution, new_residual, new_direction
```

```python
import jax
import jax.numpy as jnp
from jax import lax
from jax.sharding import PartitionSpec as P


def body(saved_acts, solution, residual, direction):
    low_dir = direction.astype(jnp.bfloat16)
    acts = lax.all_gather(saved_acts, "dp", axis=0, tiled=True)
    partial_tan = jnp.dot(acts, low_dir, preferred_element_type=jnp.float32)
    mine = lax.psum_scatter(partial_tan, "mp", scatter_dimension=0, tiled=True)
    tangent = lax.all_gather(mine.astype(jnp.bfloat16), "mp", axis=0, tiled=True)
    pulled = lax.dot_general(
        acts, tangent, (((0,), (0,)), ((), ())), preferred_element_type=jnp.float32
    )
    curved = pulled / acts.shape[0] + 1.0 * direction
    sums = jnp.stack(
        [
            jnp.sum(residual * residual),
            jnp.sum(direction * curved),
            jnp.sum(residual * curved),
            jnp.sum(curved * curved),
        ]
    )
    norm_old, along, res_curved, curved_sq = lax.psum(sums, ("dp", "mp"))
    step_size = norm_old / along
    new_residual = residual - step_size * curved
    norm_new = norm_old + step_size * (step_size * curved_sq - 2.0 * res_curved)
    new_solution = solution + step_size * direction
    new_direction = new_residual + norm_new / norm_old * direction
    return (new_solution, new_residual, new_direction)


def solution(mesh):
    return jax.shard_map(
        body,
        mesh=mesh,
        in_specs=(P("dp", "mp"), P("mp", "dp"), P("mp", "dp"), P("mp", "dp")),
        out_specs=(P("mp", "dp"), P("mp", "dp"), P("mp", "dp")),
        check_vma=False,
    )
```

```python
import jax
import jax.numpy as jnp
from jax import lax
from jax.experimental import pallas as pl
from jax.experimental.pallas import tpu as pltpu
from jax.sharding import PartitionSpec as P

RING = 4
PIECES = 3
CHUNKS = 2 * RING * PIECES
HOP = 2
LAG = [0, 1, 1 + HOP, 1 + 2 * HOP, 1 + 3 * HOP, 1 + 4 * HOP, 1 + 5 * HOP, 1 + 6 * HOP]
STEPS = CHUNKS + LAG[-1]
MESH = pl.DeviceIdType.MESH


def chunk_place(k):
    late = (k + 18) // 24
    last = (k + 6) // 24
    mid = late - last
    away = mid * (1 + 2 * (k % 2)) + last * 2
    other = (1 - late) * (k // 3) + mid * ((k // 2 + 1) % 2) + last * (k % 2)
    piece = (1 - late) * (k % 3) + mid * ((k + 2) // 4 - 2) + last * (k // 2 - 9)
    return away, other, piece


def kernel(
    acts_ref, res_ref, dir_ref, curved_ref, sums_ref,
    acts, low, tan, part, pass1, got1a, got1b, quad, got2, tiles,
    own_sem, y_send, y_recv, fwd_send, sib_send, sib_recv,
    r1_send, r1_recv, f1_send, f1_recv, r2_send, r2_recv,
    g1_send, g1_recv, g2_send, g2_recv, f2_send, f2_recv,
    sum_send, sum_recv,
):
    dp, mp = lax.axis_index("dp"), lax.axis_index("mp")
    y, c = dp // 2, dp % 2
    z, x = mp // RING, mp % RING
    block = acts_ref.shape[0]
    rows = block // PIECES
    big, small = rows // RING, rows // RING // RING
    tokens = acts.shape[0]
    p1 = x * (1 - c) + z * c
    p2 = z * (1 - c) + x * c
    turn = 1 - 2 * c

    def along_y(d):
        return (((y + d + RING) % RING) * 2 + c, mp)

    def first(d):
        return (dp, ((z + d * c + RING) % RING) * RING + (x + d * (1 - c) + RING) % RING)

    def second(d):
        return (dp, ((z + d * (1 - c)) % RING) * RING + (x + d * c) % RING)

    sibling = (y * 2 + 1 - c, mp)

    def act_rows(away, other, piece):
        who = ((y + away) % RING) * 2 + (c + other) % 2
        return pl.ds(pl.multiple_of(who * block + piece * rows, rows), rows)

    def remote(src, dst, send, recv, to):
        return pltpu.make_async_remote_copy(
            src_ref=src, dst_ref=dst, send_sem=send, recv_sem=recv,
            device_id=to, device_id_type=MESH,
        )

    barrier = pltpu.get_barrier_semaphore()

    @pl.loop(1, 16)
    def _(o):
        pl.semaphore_signal(barrier, inc=1, device_id=(dp, (mp + o) % 16), device_id_type=MESH)

    @pl.loop(1, 8)
    def _(o):
        pl.semaphore_signal(barrier, inc=1, device_id=((dp + o) % 8, mp), device_id_type=MESH)

    for j in range(PIECES):
        pltpu.make_async_copy(
            acts_ref.at[pl.ds(j * rows, rows)], acts.at[act_rows(0, 0, j)], own_sem.at[j]
        ).start()
    low[...] = dir_ref[...].astype(jnp.bfloat16)
    curved_ref[...] = jnp.zeros_like(curved_ref)
    pl.semaphore_wait(barrier, 22)

    def y_copy(j, way):
        here = acts.at[act_rows(0, 0, j)]
        arrives = 1 + 2 * way
        return remote(
            here, here, y_send.at[way, j], y_recv.at[arrives, j], along_y(2 * way - 1)
        )

    def sib_copy(away, j):
        here = acts.at[act_rows(away, 0, j)]
        return remote(here, here, sib_send.at[away, j], sib_recv.at[away, j], sibling)

    def fwd_copy(j):
        here = acts.at[act_rows((RING - turn) % RING, 0, j)]
        return remote(here, here, fwd_send.at[j], y_recv.at[2, j], along_y(turn))

    for j in range(PIECES):
        pltpu.make_async_copy(
            acts_ref.at[pl.ds(j * rows, rows)], acts.at[act_rows(0, 0, j)], own_sem.at[j]
        ).wait()
        y_copy(j, 0).start()
        y_copy(j, 1).start()
        sib_copy(0, j).start()

    def part_rows(k, slot):
        return pl.ds(pl.multiple_of(k * rows + slot * big, 16), big)

    def quad_rows(k, slot):
        return pl.ds(pl.multiple_of(k * big + slot * small, 16), small)

    def tan_rows(k, slot, sub):
        return pl.ds(pl.multiple_of(k * rows + slot * big + sub * small, 16), small)

    def big_rows(k):
        return pl.ds(pl.multiple_of(k * big, 16), big)

    def two_rows(k, o):
        return pl.ds(pl.multiple_of((k * 3 + o - 1) * small, 16), small)

    def way_of(k):
        return 1 - 2 * (k % 2)

    def r1_copy(k, which):
        s = way_of(k)
        if which == 0:
            src = part.at[part_rows(k, (p1 + 2) % RING)]
            return remote(src, pass1.at[big_rows(k)], r1_send.at[k, 0], r1_recv.at[k, 0], first(s))
        src = part.at[part_rows(k, (p1 + RING - s) % RING)]
        return remote(src, got1b.at[big_rows(k)], r1_send.at[k, 1], r1_recv.at[k, 1], first(-s))

    def f1_copy(k):
        s = way_of(k)
        src = part.at[part_rows(k, (p1 + RING + s) % RING)]
        return remote(src, got1a.at[big_rows(k)], f1_send.at[k], f1_recv.at[k], first(s))

    def r2_copy(k, o):
        src = quad.at[quad_rows(k, (p2 + o) % RING)]
        return remote(
            src, got2.at[two_rows(k, o)], r2_send.at[k, o - 1], r2_recv.at[k, o - 1], second(o)
        )

    def g1_copy(k, o, whose):
        here = tan.at[tan_rows(k, p1, whose)]
        return remote(here, here, g1_send.at[k, o - 1], g1_recv.at[k, o - 1], second(o))

    def g2_copy(k, way, whose):
        here = tan.at[part_rows(k, whose)]
        to = first(way_of(k) * (1 - 2 * way))
        return remote(here, here, g2_send.at[k, way], g2_recv.at[k, way], to)

    def f2_copy(k, whose):
        here = tan.at[part_rows(k, whose)]
        return remote(here, here, f2_send.at[k], f2_recv.at[k], first(way_of(k)))

    def arrive(k):
        away, other, piece = chunk_place(k)

        @pl.when((other == 0) & (away != 0))
        def _():
            here = acts.at[act_rows(away, 0, piece)]
            remote(
                here, here, y_send.at[0, 0], y_recv.at[away, piece], sibling
            ).wait_recv()
            sib_copy(away, piece).start()

            @pl.when(away == (RING - turn) % RING)
            def _():
                fwd_copy(piece).start()

        @pl.when(other == 1)
        def _():
            here = acts.at[act_rows(away, 1, piece)]
            remote(
                here, here, sib_send.at[0, 0], sib_recv.at[away, piece], sibling
            ).wait_recv()

    def forward_product(k):
        away, other, piece = chunk_place(k)
        product = jnp.dot(
            acts[act_rows(away, other, piece), :], low[...], preferred_element_type=jnp.float32
        )
        part[pl.ds(pl.multiple_of(k * rows, rows), rows), :] = product.astype(jnp.bfloat16)
        r1_copy(k, 0).start()
        r1_copy(k, 1).start()

    def pass_on(k):
        r1_copy(k, 0).wait_recv()
        here = part_rows(k, (p1 + RING + way_of(k)) % RING)
        part[here, :] = (
            part[here, :].astype(jnp.float32) + pass1[big_rows(k), :].astype(jnp.float32)
        ).astype(jnp.bfloat16)
        f1_copy(k).start()

    def quarter(k):
        f1_copy(k).wait_recv()
        r1_copy(k, 1).wait_recv()
        quad[big_rows(k), :] = (
            part[part_rows(k, p1), :].astype(jnp.float32)
            + got1a[big_rows(k), :].astype(jnp.float32)
            + got1b[big_rows(k), :].astype(jnp.float32)
        ).astype(jnp.bfloat16)
        for o in range(1, RING):
            r2_copy(k, o).start()

    def total(k):
        value = quad[quad_rows(k, p2), :].astype(jnp.float32)
        for o in range(1, RING):
            r2_copy(k, o).wait_recv()
            value = value + got2[two_rows(k, o), :].astype(jnp.float32)
        tan[tan_rows(k, p1, p2), :] = value.astype(jnp.bfloat16)
        for o in range(1, RING):
            g1_copy(k, o, p2).start()

    def spread(k):
        for o in range(1, RING):
            g1_copy(k, o, (p2 + RING - o) % RING).wait_recv()
        g2_copy(k, 0, p1).start()
        g2_copy(k, 1, p1).start()

    def spread_on(k):
        whose = (p1 + RING - way_of(k)) % RING
        g2_copy(k, 0, whose).wait_recv()
        f2_copy(k, whose).start()

    def back_product(k):
        s = way_of(k)
        g2_copy(k, 1, (p1 + RING + s) % RING).wait_recv()
        f2_copy(k, (p1 + 2) % RING).wait_recv()
        away, other, piece = chunk_place(k)
        t = tan[pl.ds(pl.multiple_of(k * rows, rows), rows), :]
        width = 384

        @pl.loop(0, acts.shape[1] // width)
        def _(h):
            cols = pl.ds(pl.multiple_of(h * width, width), width)
            curved_ref[cols, :] += lax.dot_general(
                acts[act_rows(away, other, piece), cols], t, (((0,), (0,)), ((), ())),
                preferred_element_type=jnp.float32,
            )

        r1_copy(k, 0).wait_send()
        r1_copy(k, 1).wait_send()
        f1_copy(k).wait_send()
        for o in range(1, RING):
            r2_copy(k, o).wait_send()
            g1_copy(k, o, p2).wait_send()
        g2_copy(k, 0, p1).wait_send()
        g2_copy(k, 1, p1).wait_send()
        f2_copy(k, (p1 + RING - s) % RING).wait_send()

    stages = [
        (2, pass_on), (3, quarter), (4, total), (5, spread), (6, spread_on),
        (0, arrive), (1, forward_product), (7, back_product),
    ]

    @pl.loop(0, STEPS)
    def _(step):
        for at, stage in stages:
            k = step - LAG[at]

            @pl.when((k >= 0) & (k < CHUNKS))
            def _(k=k, stage=stage):
                stage(k)

    for j in range(PIECES):
        y_copy(j, 0).wait_send()
        y_copy(j, 1).wait_send()
        fwd_copy(j).wait_send()
        for away in range(RING):
            sib_copy(away, j).wait_send()

    direction, residual = dir_ref[...], res_ref[...]
    curved = curved_ref[...] / tokens + 1.0 * direction
    curved_ref[...] = curved

    def line(v):
        one = jnp.sum(jnp.sum(v, axis=0, keepdims=True), axis=1, keepdims=True)
        return jnp.broadcast_to(one, (1, 128))

    mine = jnp.concatenate(
        [line(residual * residual), line(direction * curved), line(residual * curved),
         line(curved * curved), jnp.zeros((4, 128), jnp.float32)], axis=0,
    )
    tiles[mp] = mine

    def plane_copy(o, whose):
        here = tiles.at[whose]
        return remote(here, here, sum_send.at[o], sum_recv.at[o], (dp, (mp + o) % 16))

    def column_copy(o, whose):
        here = tiles.at[16 + whose]
        return remote(here, here, sum_send.at[16 + o], sum_recv.at[16 + o], ((dp + o) % 8, mp))

    @pl.loop(1, 16)
    def _(o):
        plane_copy(o, mp).start()

    @pl.loop(1, 16)
    def _(o):
        plane_copy(o, (mp + 16 - o) % 16).wait_recv()

    subtotal = tiles[0]
    for i in range(1, 16):
        subtotal = subtotal + tiles[i]
    tiles[16 + dp] = subtotal

    @pl.loop(1, 8)
    def _(o):
        column_copy(o, dp).start()

    @pl.loop(1, 8)
    def _(o):
        column_copy(o, (dp + 8 - o) % 8).wait_recv()

    whole = tiles[16]
    for i in range(1, 8):
        whole = whole + tiles[16 + i]
    sums_ref[...] = whole

    @pl.loop(1, 16)
    def _(o):
        plane_copy(o, mp).wait_send()

    @pl.loop(1, 8)
    def _(o):
        column_copy(o, dp).wait_send()


def curvature(saved_acts, residual, direction):
    block, hidden = saved_acts.shape
    columns = direction.shape[1]
    rows = block // PIECES
    big, small = rows // RING, rows // RING // RING
    bf16, f32 = jnp.bfloat16, jnp.float32
    dma = pltpu.SemaphoreType.DMA
    vmem = pl.BlockSpec(memory_space=pltpu.VMEM)
    return pl.pallas_call(
        kernel,
        out_shape=(
            jax.ShapeDtypeStruct((hidden, columns), f32),
            jax.ShapeDtypeStruct((8, 128), f32),
        ),
        in_specs=[pl.BlockSpec(memory_space=pl.ANY), vmem, vmem],
        out_specs=(vmem, vmem),
        scratch_shapes=[
            pltpu.VMEM((8 * block, hidden), bf16),
            pltpu.VMEM((hidden, columns), bf16),
            pltpu.VMEM((CHUNKS * rows, columns), bf16),
            pltpu.VMEM((CHUNKS * rows, columns), bf16),
            pltpu.VMEM((CHUNKS * big, columns), bf16),
            pltpu.VMEM((CHUNKS * big, columns), bf16),
            pltpu.VMEM((CHUNKS * big, columns), bf16),
            pltpu.VMEM((CHUNKS * big, columns), bf16),
            pltpu.VMEM((CHUNKS * 3 * small, columns), bf16),
            pltpu.VMEM((24, 8, 128), f32),
            dma((PIECES,)), dma((2, PIECES)), dma((RING, PIECES)), dma((PIECES,)),
            dma((RING, PIECES)), dma((RING, PIECES)),
            dma((CHUNKS, 2)), dma((CHUNKS, 2)), dma((CHUNKS,)), dma((CHUNKS,)),
            dma((CHUNKS, 3)), dma((CHUNKS, 3)), dma((CHUNKS, 3)), dma((CHUNKS, 3)),
            dma((CHUNKS, 2)), dma((CHUNKS, 2)), dma((CHUNKS,)), dma((CHUNKS,)),
            dma((24,)), dma((24,)),
        ],
        compiler_params=pltpu.CompilerParams(
            collective_id=0, has_side_effects=True, vmem_limit_bytes=62 * 2**20
        ),
        cost_estimate=pl.CostEstimate(
            flops=32 * block * hidden * columns, bytes_accessed=16 * 2**20, transcendentals=0
        ),
    )(saved_acts, residual, direction)


def body(saved_acts, solution, residual, direction):
    curved, sums = curvature(saved_acts, residual, direction)
    norm_old, along, res_curved, curved_sq = sums[0, 0], sums[1, 0], sums[2, 0], sums[3, 0]
    step_size = norm_old / along
    new_residual = residual - step_size * curved
    norm_new = norm_old + step_size * (step_size * curved_sq - 2.0 * res_curved)
    new_solution = solution + step_size * direction
    new_direction = new_residual + norm_new / norm_old * direction
    return (new_solution, new_residual, new_direction)


def solution(mesh):
    return jax.shard_map(
        body,
        mesh=mesh,
        in_specs=(P("dp", "mp"), P("mp", "dp"), P("mp", "dp"), P("mp", "dp")),
        out_specs=(P("mp", "dp"), P("mp", "dp"), P("mp", "dp")),
        check_vma=False,
    )
```

```python
import jax
import jax.numpy as jnp
from jax import lax
from jax.experimental import pallas as pl
from jax.experimental.pallas import tpu as pltpu
from jax.sharding import PartitionSpec as P

RING = 4
PIECES = 3
CHUNKS = 2 * RING * PIECES
PAIRS = CHUNKS // 2
HOP = 3
SEND_AT = (6, 12)
LAG = [0, 1, 1 + HOP, 1 + 2 * HOP, 1 + 3 * HOP, 1 + 4 * HOP, 1 + 5 * HOP, 1 + 6 * HOP]
REST = 6
STEPS = CHUNKS + REST + LAG[-1]
MESH = pl.DeviceIdType.MESH


def chunk_place(k):
    late = (k + 18) // 24
    last = (k + 6) // 24
    mid = late - last
    away = mid * (1 + 2 * (k % 2)) + last * 2
    other = (1 - late) * (k // 3) + mid * ((k // 2 + 1) % 2) + last * (k % 2)
    piece = (1 - late) * (k % 3) + mid * ((k + 2) // 4 - 2) + last * (k // 2 - 9)
    return away, other, piece


def kernel(
    acts_ref, res_ref, dir_ref, curved_ref, sums_ref,
    acts, low, tan, part, pass1, got1a, got1b, quad, got2, tiles, dir_here, res_here,
    own_sem, y_send, y_recv, fwd_send, sib_send, sib_recv,
    sent, r1_recv, f1_recv, r2_recv, g1_recv, g2_recv, f2_recv,
    sum_send, sum_recv,
):
    dp, mp = lax.axis_index("dp"), lax.axis_index("mp")
    y, c = dp // 2, dp % 2
    z, x = mp // RING, mp % RING
    block = acts_ref.shape[0]
    rows = block // PIECES
    cols = low.shape[0]
    big = cols // RING
    lanes = 2 * rows // RING
    tokens = acts.shape[0]
    p1 = x * (1 - c) + z * c
    p2 = z * (1 - c) + x * c
    turn = 1 - 2 * c

    def along_y(d):
        return (((y + d + RING) % RING) * 2 + c, mp)

    def first(d):
        return (dp, ((z + d * c + RING) % RING) * RING + (x + d * (1 - c) + RING) % RING)

    def second(d):
        return (dp, ((z + d * (1 - c)) % RING) * RING + (x + d * c) % RING)

    sibling = (y * 2 + 1 - c, mp)

    def act_rows(away, other, piece):
        who = ((y + away) % RING) * 2 + (c + other) % 2
        return pl.ds(pl.multiple_of(who * block + piece * rows, rows), rows)

    def remote(src, dst, send, recv, to):
        return pltpu.make_async_remote_copy(
            src_ref=src, dst_ref=dst, send_sem=send, recv_sem=recv,
            device_id=to, device_id_type=MESH,
        )

    def own_copy(j):
        return pltpu.make_async_copy(
            acts_ref.at[pl.ds(j * rows, rows)], acts.at[act_rows(0, 0, j)], own_sem.at[j]
        )

    load_dir = pltpu.make_async_copy(dir_ref, dir_here, own_sem.at[PIECES])
    load_res = pltpu.make_async_copy(res_ref, res_here, own_sem.at[PIECES + 1])
    load_dir.start()
    for j in range(PIECES):
        own_copy(j).start()
    load_res.start()
    barrier = pltpu.get_barrier_semaphore()

    @pl.loop(1, 16)
    def _(o):
        pl.semaphore_signal(barrier, inc=1, device_id=(dp, (mp + o) % 16), device_id_type=MESH)

    @pl.loop(1, 8)
    def _(o):
        pl.semaphore_signal(barrier, inc=1, device_id=((dp + o) % 8, mp), device_id_type=MESH)

    load_dir.wait()
    low[...] = dir_here[...].astype(jnp.bfloat16)
    curved_ref[...] = jnp.zeros_like(curved_ref)
    pl.semaphore_wait(barrier, 22)

    def y_copy(j, way):
        here = acts.at[act_rows(0, 0, j)]
        arrives = 1 + 2 * way
        return remote(
            here, here, y_send.at[way, j], y_recv.at[arrives, j], along_y(2 * way - 1)
        )

    def sib_copy(away, j):
        here = acts.at[act_rows(away, 0, j)]
        return remote(here, here, sib_send.at[away, j], sib_recv.at[away, j], sibling)

    def fwd_copy(j):
        here = acts.at[act_rows((RING - turn) % RING, 0, j)]
        return remote(here, here, fwd_send.at[j], y_recv.at[2, j], along_y(turn))

    for j in range(PIECES):
        own_copy(j).wait()
        sib_copy(0, j).start()
        if j == 0:
            y_copy(j, 0).start()
            y_copy(j, 1).start()

    def slot_rows(slot):
        return pl.ds(pl.multiple_of(slot * big, 16), big)

    def lane(slot):
        return pl.ds(pl.multiple_of(slot * lanes, lanes), lanes)

    def way_of(k):
        return 1 - 2 * (k % 2)

    def r1_copy(k, which):
        s = way_of(k)
        if which == 0:
            src = part.at[k, slot_rows((p1 + 2) % RING)]
            return remote(src, pass1.at[k], sent.at[k // 2], r1_recv.at[k, 0], first(s))
        src = part.at[k, slot_rows((p1 + RING - s) % RING)]
        return remote(src, got1b.at[k], sent.at[k // 2], r1_recv.at[k, 1], first(-s))

    def f1_copy(k):
        s = way_of(k)
        src = part.at[k, slot_rows((p1 + RING + s) % RING)]
        return remote(src, got1a.at[k], sent.at[k // 2], f1_recv.at[k], first(s))

    def r2_copy(m, o):
        src = quad.at[m, :, lane((p2 + o) % RING)]
        return remote(src, got2.at[m, o - 1], sent.at[m], r2_recv.at[m], second(o))

    def g1_copy(m, o):
        here = tan.at[m, slot_rows(p1), lane(p2)]
        return remote(here, here, sent.at[m], g1_recv.at[m], second(o))

    def g2_copy(m, way, whose):
        here = tan.at[m, slot_rows(whose)]
        to = first(way_of(m) * (1 - 2 * way))
        return remote(here, here, sent.at[m], g2_recv.at[m, way], to)

    def f2_copy(m, whose):
        here = tan.at[m, slot_rows(whose)]
        return remote(here, here, sent.at[m], f2_recv.at[m], first(way_of(m)))

    def wait_all(sem, some):
        pltpu.make_async_copy(some, some, sem).wait()

    def arrive(k):
        away, other, piece = chunk_place(k)

        @pl.when((other == 0) & (away != 0))
        def _():
            here = acts.at[act_rows(away, 0, piece)]
            remote(
                here, here, y_send.at[0, 0], y_recv.at[away, piece], sibling
            ).wait_recv()
            sib_copy(away, piece).start()

            @pl.when(away == (RING - turn) % RING)
            def _():
                fwd_copy(piece).start()

        @pl.when(other == 1)
        def _():
            here = acts.at[act_rows(away, 1, piece)]
            remote(
                here, here, sib_send.at[0, 0], sib_recv.at[away, piece], sibling
            ).wait_recv()

    def forward_product(k):
        product = lax.dot_general(
            low[...], acts[act_rows(*chunk_place(k)), :], (((1,), (1,)), ((), ())),
            preferred_element_type=jnp.float32,
        )
        part[k] = product.astype(jnp.bfloat16)
        r1_copy(k, 0).start()
        r1_copy(k, 1).start()

    def pass_on(k):
        r1_copy(k, 0).wait_recv()
        here = slot_rows((p1 + RING + way_of(k)) % RING)
        part[k, here, :] = (
            part[k, here, :].astype(jnp.float32) + pass1[k].astype(jnp.float32)
        ).astype(jnp.bfloat16)
        f1_copy(k).start()

    def quarter(k):
        f1_copy(k).wait_recv()
        r1_copy(k, 1).wait_recv()
        half = pl.ds(pl.multiple_of((k % 2) * rows, rows), rows)
        quad[k // 2, :, half] = (
            part[k, slot_rows(p1), :].astype(jnp.float32)
            + got1a[k].astype(jnp.float32)
            + got1b[k].astype(jnp.float32)
        ).astype(jnp.bfloat16)

        @pl.when(k % 2 == 1)
        def _():
            for o in range(1, RING):
                r2_copy(k // 2, o).start()

    def total(m):
        wait_all(r2_recv.at[m], got2.at[m])
        value = quad[m, :, lane(p2)].astype(jnp.float32)
        for o in range(1, RING):
            value = value + got2[m, o - 1].astype(jnp.float32)
        tan[m, slot_rows(p1), lane(p2)] = value.astype(jnp.bfloat16)
        for o in range(1, RING):
            g1_copy(m, o).start()

    def spread(m):
        wait_all(g1_recv.at[m], got2.at[m])
        g2_copy(m, 0, p1).start()
        g2_copy(m, 1, p1).start()

    def spread_on(m):
        whose = (p1 + RING - way_of(m)) % RING
        g2_copy(m, 0, whose).wait_recv()
        f2_copy(m, whose).start()

    def back_product(m):
        g2_copy(m, 1, (p1 + RING + way_of(m)) % RING).wait_recv()
        f2_copy(m, (p1 + 2) % RING).wait_recv()

        @pl.loop(0, acts.shape[1] // WIDE)
        def _(h):
            at = pl.ds(pl.multiple_of(h * WIDE, WIDE), WIDE)
            curved_ref[:, at] += jnp.dot(
                tan[m, :, 0:rows], acts[act_rows(*chunk_place(2 * m)), at],
                preferred_element_type=jnp.float32,
            ) + jnp.dot(
                tan[m, :, rows : 2 * rows], acts[act_rows(*chunk_place(2 * m + 1)), at],
                preferred_element_type=jnp.float32,
            )

        wait_all(sent.at[m], part.at[2 * m])
        wait_all(sent.at[m], part.at[2 * m, pl.ds(0, 2 * big)])
        wait_all(sent.at[m], got2.at[m])
        wait_all(sent.at[m], got2.at[m])
        wait_all(sent.at[m], tan.at[m, pl.ds(0, 3 * big)])

    stages = [
        (2, pass_on, 1), (3, quarter, 1), (4, total, 2), (5, spread, 2), (6, spread_on, 2),
        (0, arrive, 1), (1, forward_product, 1), (7, back_product, 2),
    ]

    @pl.loop(0, STEPS)
    def _(step):
        for j, at in ((1, SEND_AT[0]), (2, SEND_AT[1])):

            @pl.when(step == at)
            def _(j=j):
                y_copy(j, 0).start()
                y_copy(j, 1).start()

        for at, stage, every in stages:
            turn_of = step - LAG[at]
            rested = (turn_of + 64 - 2 * PIECES - REST) // 64
            k = turn_of - rested * REST

            @pl.when(
                (k >= 0) & (k < CHUNKS) & ((rested == 1) | (k < 2 * PIECES))
                & (k % every == every - 1)
            )
            def _(k=k, stage=stage, every=every):
                stage(k // every)

    for j in range(PIECES):
        y_copy(j, 0).wait_send()
        y_copy(j, 1).wait_send()
        fwd_copy(j).wait_send()
        for away in range(RING):
            sib_copy(away, j).wait_send()

    load_res.wait()
    direction, residual = dir_here[...], res_here[...]
    curved = curved_ref[...] / tokens + 1.0 * direction
    curved_ref[...] = curved

    def total_of(v):
        return jnp.sum(jnp.sum(v, axis=0, keepdims=True), axis=1, keepdims=True)

    place = lax.broadcasted_iota(jnp.int32, (1, 128), 1)
    mine = jnp.zeros((1, 128), jnp.float32)
    for i, (a, b) in enumerate(
        ((residual, residual), (direction, curved), (residual, curved), (curved, curved))
    ):
        mine = jnp.where(place == i, total_of(a * b), mine)
    tiles[mp] = mine

    def plane_copy(o, whose):
        here = tiles.at[whose]
        return remote(here, here, sum_send.at[o], sum_recv.at[o], (dp, (mp + o) % 16))

    def column_copy(o, whose):
        here = tiles.at[16 + whose]
        return remote(here, here, sum_send.at[16 + o], sum_recv.at[16 + o], ((dp + o) % 8, mp))

    @pl.loop(1, 16)
    def _(o):
        plane_copy(o, mp).start()

    @pl.loop(1, 16)
    def _(o):
        plane_copy(o, (mp + 16 - o) % 16).wait_recv()

    subtotal = tiles[0]
    for i in range(1, 16):
        subtotal = subtotal + tiles[i]
    tiles[16 + dp] = subtotal

    @pl.loop(1, 8)
    def _(o):
        column_copy(o, dp).start()

    @pl.loop(1, 8)
    def _(o):
        column_copy(o, (dp + 8 - o) % 8).wait_recv()

    whole = tiles[16]
    for i in range(1, 8):
        whole = whole + tiles[16 + i]
    sums_ref[...] = jnp.broadcast_to(whole, (8, 128))

    @pl.loop(1, 16)
    def _(o):
        plane_copy(o, mp).wait_send()

    @pl.loop(1, 8)
    def _(o):
        column_copy(o, dp).wait_send()


WIDE = 384


def curvature(saved_acts, residual, direction):
    block, hidden = saved_acts.shape
    columns = direction.shape[0]
    rows = block // PIECES
    big, lanes = columns // RING, 2 * rows // RING
    bf16, f32 = jnp.bfloat16, jnp.float32
    dma = pltpu.SemaphoreType.DMA
    vmem = pl.BlockSpec(memory_space=pltpu.VMEM)
    return pl.pallas_call(
        kernel,
        out_shape=(
            jax.ShapeDtypeStruct((columns, hidden), f32),
            jax.ShapeDtypeStruct((8, 128), f32),
        ),
        in_specs=[pl.BlockSpec(memory_space=pltpu.HBM)] * 3,
        out_specs=(vmem, vmem),
        scratch_shapes=[
            pltpu.VMEM((8 * block, hidden), bf16),
            pltpu.VMEM((columns, hidden), bf16),
            pltpu.VMEM((PAIRS, columns, 2 * rows), bf16),
            pltpu.VMEM((CHUNKS, columns, rows), bf16),
            pltpu.VMEM((CHUNKS, big, rows), bf16),
            pltpu.VMEM((CHUNKS, big, rows), bf16),
            pltpu.VMEM((CHUNKS, big, rows), bf16),
            pltpu.VMEM((PAIRS, big, 2 * rows), bf16),
            pltpu.VMEM((PAIRS, 3, big, lanes), bf16),
            pltpu.VMEM((24, 1, 128), f32),
            pltpu.VMEM((columns, hidden), f32),
            pltpu.VMEM((columns, hidden), f32),
            dma((PIECES + 2,)), dma((2, PIECES)), dma((RING, PIECES)), dma((PIECES,)),
            dma((RING, PIECES)), dma((RING, PIECES)),
            dma((PAIRS,)), dma((CHUNKS, 2)), dma((CHUNKS,)), dma((PAIRS,)), dma((PAIRS,)),
            dma((PAIRS, 2)), dma((PAIRS,)),
            dma((24,)), dma((24,)),
        ],
        compiler_params=pltpu.CompilerParams(
            collective_id=0, has_side_effects=True, vmem_limit_bytes=46 * 2**20
        ),
        cost_estimate=pl.CostEstimate(
            flops=32 * block * hidden * columns, bytes_accessed=16 * 2**20, transcendentals=0
        ),
    )(saved_acts, residual, direction)


def finish_kernel(sums_ref, curved_ref, sol_ref, res_ref, dir_ref, *refs):
    outs, here, sems = refs[:3], refs[3:6], refs[6]
    norm_old, along = sums_ref[0:1, 0:1], sums_ref[0:1, 1:2]
    res_curved, curved_sq = sums_ref[0:1, 2:3], sums_ref[0:1, 3:4]
    step_size = norm_old / along
    norm_new = norm_old + step_size * (step_size * curved_sq - 2.0 * res_curved)
    growth = norm_new / norm_old
    blocks = 4
    size = curved_ref.shape[0] // blocks
    copies = []
    for i in range(blocks):
        at = pl.ds(i * size, size)
        direction = dir_ref[at, :]
        new_residual = res_ref[at, :] - step_size * curved_ref[at, :]
        here[0][at, :] = sol_ref[at, :] + step_size * direction
        here[1][at, :] = new_residual
        here[2][at, :] = new_residual + growth * direction
        for o in range(3):
            copy = pltpu.make_async_copy(here[o].at[at], outs[o].at[at], sems.at[o, i])
            copy.start()
            copies.append(copy)
    for copy in copies:
        copy.wait()


def finish(sums, curved, solution, residual, direction):
    vmem = pl.BlockSpec(memory_space=pltpu.VMEM)
    field = jax.ShapeDtypeStruct(curved.shape, jnp.float32)
    return pl.pallas_call(
        finish_kernel,
        out_shape=(field,) * 3,
        in_specs=[vmem] * 5,
        out_specs=(pl.BlockSpec(memory_space=pltpu.HBM),) * 3,
        scratch_shapes=[pltpu.VMEM(curved.shape, jnp.float32)] * 3
        + [pltpu.SemaphoreType.DMA((3, 4))],
        compiler_params=pltpu.CompilerParams(vmem_limit_bytes=40 * 2**20),
    )(sums, curved, solution, residual, direction)


def body(saved_acts, solution, residual, direction):
    solution, residual, direction = solution.T, residual.T, direction.T
    curved, sums = curvature(saved_acts, residual, direction)
    outs = finish(sums, curved, solution, residual, direction)
    return tuple(out.T for out in outs)


def solution(mesh):
    return jax.shard_map(
        body,
        mesh=mesh,
        in_specs=(P("dp", "mp"), P("mp", "dp"), P("mp", "dp"), P("mp", "dp")),
        out_specs=(P("mp", "dp"), P("mp", "dp"), P("mp", "dp")),
        check_vma=False,
    )
```

```python
import jax
import jax.numpy as jnp
from jax import lax
from jax.experimental import pallas as pl
from jax.experimental.pallas import tpu as pltpu
from jax.sharding import PartitionSpec as P

RING = 4
PIECES = 3
CHUNKS = 2 * RING * PIECES
PAIRS = CHUNKS // 2
SENDS = ((1, 0, 0), (11, 1, 1), (13, 1, 0), (14, 2, 1), (25, 2, 0))
LAG = (1, 5, 9, 12, 16, 23, 29)
RESTS = ((6, 7), (10, 9), (14, 1), (18, 2))
STEPS = CHUNKS + sum(rest for _, rest in RESTS) + LAG[-1]
MESH = pl.DeviceIdType.MESH


def chunk_place(k, turn):
    late, last = lax.div(k + 18, 24), lax.div(k + 6, 24)
    mid = late - last
    away = mid * (2 + turn * (1 - 2 * (lax.rem(lax.div(lax.rem(k + 3, 4), 2), 2)))) + last * 2
    other = (1 - late) * lax.div(k, 3) + (mid + last) * lax.rem(k, 2)
    piece = (1 - late) * lax.rem(k, 3) + mid * (lax.div(k + 2, 4) - 2)
    piece += last * (lax.div(k, 2) - 9)
    return away, other, piece


def kernel(
    acts_ref, res_ref, dir_ref, curved_ref, sums_ref,
    acts, low, tan, part, pass1, got1a, got1b, quad, got2, tiles, dir_here, res_here,
    own_sem, y_send, y_recv, fwd_send, sib_send, sib_recv,
    sent, r1_recv, f1_recv, r2_recv, g1_recv, g2_recv, f2_recv,
    sum_send, sum_recv,
):
    dp, mp = lax.axis_index("dp"), lax.axis_index("mp")
    y, c = dp // 2, dp % 2
    z, x = mp // RING, mp % RING
    block = acts_ref.shape[0]
    rows = block // PIECES
    cols = low.shape[0]
    big = cols // RING
    lanes = 2 * rows // RING
    tokens = acts.shape[0]
    p1 = x * (1 - c) + z * c
    p2 = z * (1 - c) + x * c
    turn = 1 - 2 * c

    def along_y(d):
        return (((y + d + RING) % RING) * 2 + c, mp)

    def plane(to_x, to_z):
        return lax.rem(z + to_z + RING, RING) * RING + lax.rem(x + to_x + RING, RING)

    up, down = plane(1 - c, c), plane(c - 1, -c)
    second = [plane(o * c, o * (1 - c)) for o in range(RING)]
    up_slot, down_slot, far_slot = (lax.rem(p1 + o, RING) for o in (1, 3, 2))
    second_slot = [lax.rem(p2 + o, RING) for o in range(RING)]

    def ahead(k):
        return up + (down - up) * lax.rem(k, 2)

    def behind(k):
        return down + (up - down) * lax.rem(k, 2)

    def ahead_slot(k):
        return up_slot + (down_slot - up_slot) * lax.rem(k, 2)

    def behind_slot(k):
        return down_slot + (up_slot - down_slot) * lax.rem(k, 2)

    sibling = (y * 2 + 1 - c, mp)

    def act_rows(away, other, piece):
        who = lax.rem(y + away, RING) * 2 + lax.rem(c + other, 2)
        return pl.ds(pl.multiple_of(who * block + piece * rows, rows), rows)

    def remote(src, dst, send, recv, to):
        return pltpu.make_async_remote_copy(
            src_ref=src, dst_ref=dst, send_sem=send, recv_sem=recv,
            device_id=to, device_id_type=MESH,
        )

    def own_copy(j):
        return pltpu.make_async_copy(
            acts_ref.at[pl.ds(j * rows, rows)], acts.at[act_rows(0, 0, j)], own_sem.at[j]
        )

    load_dir = pltpu.make_async_copy(dir_ref, dir_here, own_sem.at[PIECES])
    load_res = pltpu.make_async_copy(res_ref, res_here, own_sem.at[PIECES + 1])
    load_dir.start()
    for j in range(PIECES):
        own_copy(j).start()
    load_res.start()
    barrier = pltpu.get_barrier_semaphore()

    @pl.loop(1, 16)
    def _(o):
        pl.semaphore_signal(barrier, inc=1, device_id=(dp, (mp + o) % 16), device_id_type=MESH)

    @pl.loop(1, 8)
    def _(o):
        pl.semaphore_signal(barrier, inc=1, device_id=((dp + o) % 8, mp), device_id_type=MESH)

    load_dir.wait()
    low[...] = dir_here[...].astype(jnp.bfloat16)
    pl.semaphore_wait(barrier, 22)

    def y_copy(j, way):
        here = acts.at[act_rows(0, 0, j)]
        arrives = 1 + 2 * way
        return remote(
            here, here, y_send.at[way, j], y_recv.at[arrives, j], along_y(2 * way - 1)
        )

    def sib_copy(away, j):
        here = acts.at[act_rows(away, 0, j)]
        return remote(here, here, sib_send.at[away, j], sib_recv.at[away, j], sibling)

    def fwd_copy(j):
        here = acts.at[act_rows((RING - turn) % RING, 0, j)]
        return remote(here, here, fwd_send.at[j], y_recv.at[2, j], along_y(turn))

    for j in range(PIECES):
        own_copy(j).wait()
        if j == 0:
            y_copy(j, 1 - c).start()
        sib_copy(0, j).start()
    curved_ref[...] = jnp.zeros_like(curved_ref)

    def slot_rows(slot):
        return pl.ds(pl.multiple_of(slot * big, 16), big)

    def lane(slot):
        return pl.ds(pl.multiple_of(slot * lanes, lanes), lanes)

    def r1_copy(k, which):
        done = sent.at[lax.div(k, 2)]
        if which == 0:
            src = part.at[k, slot_rows(far_slot)]
            return remote(src, pass1.at[k], done, r1_recv.at[k, 0], (dp, ahead(k)))
        src = part.at[k, slot_rows(behind_slot(k))]
        return remote(src, got1b.at[k], done, r1_recv.at[k, 1], (dp, behind(k)))

    def f1_copy(k):
        src = part.at[k, slot_rows(ahead_slot(k))]
        return remote(src, got1a.at[k], sent.at[lax.div(k, 2)], f1_recv.at[k], (dp, ahead(k)))

    def r2_copy(m, o):
        src = quad.at[m, :, lane(second_slot[o])]
        return remote(src, got2.at[m, o - 1], sent.at[m], r2_recv.at[m], (dp, second[o]))

    def g1_copy(m, o):
        here = tan.at[m, slot_rows(p1), lane(p2)]
        return remote(here, here, sent.at[m], g1_recv.at[m], (dp, second[o]))

    def g2_copy(m, way, whose):
        here = tan.at[m, slot_rows(whose)]
        to = behind(m) if way else ahead(m)
        return remote(here, here, sent.at[m], g2_recv.at[m, way], (dp, to))

    def f2_copy(m, whose):
        here = tan.at[m, slot_rows(whose)]
        return remote(here, here, sent.at[m], f2_recv.at[m], (dp, ahead(m)))

    def wait_all(sem, some):
        pltpu.make_async_copy(some, some, sem).wait()

    def arrive(k):
        away, other, piece = chunk_place(k, turn)

        @pl.when((other == 0) & (away != 0))
        def _():
            here = acts.at[act_rows(away, 0, piece)]
            remote(
                here, here, y_send.at[0, 0], y_recv.at[away, piece], sibling
            ).wait_recv()
            sib_copy(away, piece).start()

            @pl.when(away == (RING - turn) % RING)
            def _():
                fwd_copy(piece).start()

        @pl.when(other == 1)
        def _():
            here = acts.at[act_rows(away, 1, piece)]
            remote(
                here, here, sib_send.at[0, 0], sib_recv.at[away, piece], sibling
            ).wait_recv()

    def forward_product(k):
        product = lax.dot_general(
            low[...], acts[act_rows(*chunk_place(k, turn)), :], (((1,), (1,)), ((), ())),
            preferred_element_type=jnp.float32,
        )
        part[k] = product.astype(jnp.bfloat16)
        r1_copy(k, 0).start()
        r1_copy(k, 1).start()

    def pass_on(k):
        r1_copy(k, 0).wait_recv()
        here = slot_rows(ahead_slot(k))
        part[k, here, :] = (
            part[k, here, :].astype(jnp.float32) + pass1[k].astype(jnp.float32)
        ).astype(jnp.bfloat16)
        f1_copy(k).start()

    def quarter(k):
        f1_copy(k).wait_recv()
        r1_copy(k, 1).wait_recv()
        m, odd = lax.div(k, 2), lax.rem(k, 2)
        half = pl.ds(pl.multiple_of(odd * rows, rows), rows)
        quad[m, :, half] = (
            part[k, slot_rows(p1), :].astype(jnp.float32)
            + got1a[k].astype(jnp.float32)
            + got1b[k].astype(jnp.float32)
        ).astype(jnp.bfloat16)

        @pl.when(odd == 1)
        def _():
            for o in range(1, RING):
                r2_copy(m, o).start()

    def total(m):
        wait_all(r2_recv.at[m], got2.at[m])
        value = quad[m, :, lane(p2)].astype(jnp.float32)
        for o in range(1, RING):
            value = value + got2[m, o - 1].astype(jnp.float32)
        tan[m, slot_rows(p1), lane(p2)] = value.astype(jnp.bfloat16)
        for o in range(1, RING):
            g1_copy(m, o).start()

    def spread(m):
        wait_all(g1_recv.at[m], got2.at[m])
        g2_copy(m, 0, p1).start()
        g2_copy(m, 1, p1).start()

    def spread_on(m):
        whose = behind_slot(m)
        g2_copy(m, 0, whose).wait_recv()
        f2_copy(m, whose).start()

    def back_product(m):
        g2_copy(m, 1, ahead_slot(m)).wait_recv()
        f2_copy(m, far_slot).wait_recv()

        @pl.loop(0, acts.shape[1] // WIDE)
        def _(h):
            at = pl.ds(pl.multiple_of(h * WIDE, WIDE), WIDE)
            curved_ref[:, at] += jnp.dot(
                tan[m, :, 0:rows], acts[act_rows(*chunk_place(2 * m, turn)), at],
                preferred_element_type=jnp.float32,
            ) + jnp.dot(
                tan[m, :, rows : 2 * rows], acts[act_rows(*chunk_place(2 * m + 1, turn)), at],
                preferred_element_type=jnp.float32,
            )

        wait_all(sent.at[m], part.at[2 * m])
        wait_all(sent.at[m], part.at[2 * m, pl.ds(0, 2 * big)])
        wait_all(sent.at[m], got2.at[m])
        wait_all(sent.at[m], got2.at[m])
        wait_all(sent.at[m], tan.at[m, pl.ds(0, 3 * big)])

    stages = [
        (LAG[5], spread_on, 2), (LAG[4], spread, 2), (LAG[3], total, 2), (LAG[2], quarter, 1),
        (LAG[1], pass_on, 1), (LAG[0], arrive, 1), (LAG[0], forward_product, 1),
        (LAG[6], back_product, 2),
    ]

    @pl.loop(0, STEPS)
    def _(step):
        for at, j, way in SENDS:

            @pl.when(step == at)
            def _(j=j, way=way):
                y_copy(j, (way + c) % 2).start()

        for lag, stage, every in stages:
            turn_of = step - lag
            k, go, begin = turn_of, turn_of >= 0, 0
            for at, rest in RESTS:
                go &= (turn_of < at + begin) | (turn_of >= at + begin + rest)
                begin += rest
                k = jnp.where(turn_of >= at + begin, turn_of - begin, k)
            go &= turn_of < CHUNKS + begin
            if every == 2:
                go &= lax.rem(k, 2) == 1

            @pl.when(go)
            def _(k=k, stage=stage, every=every):
                stage(lax.div(k, every))

    for j in range(PIECES):
        y_copy(j, 0).wait_send()
        y_copy(j, 1).wait_send()
        fwd_copy(j).wait_send()
        for away in range(RING):
            sib_copy(away, j).wait_send()

    load_res.wait()
    direction, residual = dir_here[...], res_here[...]
    curved = curved_ref[...] / tokens + 1.0 * direction
    curved_ref[...] = curved

    def total_of(v):
        return jnp.sum(jnp.sum(v, axis=0, keepdims=True), axis=1, keepdims=True)

    place = lax.broadcasted_iota(jnp.int32, (1, 128), 1)
    mine = jnp.zeros((1, 128), jnp.float32)
    for i, (a, b) in enumerate(
        ((residual, residual), (direction, curved), (residual, curved), (curved, curved))
    ):
        mine = jnp.where(place == i, total_of(a * b), mine)
    tiles[mp] = mine

    def plane_copy(o, whose):
        here = tiles.at[whose]
        return remote(here, here, sum_send.at[o], sum_recv.at[o], (dp, (mp + o) % 16))

    def column_copy(o, whose):
        here = tiles.at[16 + whose]
        return remote(here, here, sum_send.at[16 + o], sum_recv.at[16 + o], ((dp + o) % 8, mp))

    @pl.loop(1, 16)
    def _(o):
        plane_copy(o, mp).start()

    @pl.loop(1, 16)
    def _(o):
        plane_copy(o, (mp + 16 - o) % 16).wait_recv()

    subtotal = tiles[0]
    for i in range(1, 16):
        subtotal = subtotal + tiles[i]
    tiles[16 + dp] = subtotal

    @pl.loop(1, 8)
    def _(o):
        column_copy(o, dp).start()

    @pl.loop(1, 8)
    def _(o):
        column_copy(o, (dp + 8 - o) % 8).wait_recv()

    whole = tiles[16]
    for i in range(1, 8):
        whole = whole + tiles[16 + i]
    sums_ref[...] = jnp.broadcast_to(whole, (8, 128))

    @pl.loop(1, 16)
    def _(o):
        plane_copy(o, mp).wait_send()

    @pl.loop(1, 8)
    def _(o):
        column_copy(o, dp).wait_send()


WIDE = 384


def curvature(saved_acts, residual, direction):
    block, hidden = saved_acts.shape
    columns = direction.shape[0]
    rows = block // PIECES
    big, lanes = columns // RING, 2 * rows // RING
    bf16, f32 = jnp.bfloat16, jnp.float32
    dma = pltpu.SemaphoreType.DMA
    vmem = pl.BlockSpec(memory_space=pltpu.VMEM)
    return pl.pallas_call(
        kernel,
        out_shape=(
            jax.ShapeDtypeStruct((columns, hidden), f32),
            jax.ShapeDtypeStruct((8, 128), f32),
        ),
        in_specs=[pl.BlockSpec(memory_space=pltpu.HBM)] * 3,
        out_specs=(vmem, vmem),
        scratch_shapes=[
            pltpu.VMEM((8 * block, hidden), bf16),
            pltpu.VMEM((columns, hidden), bf16),
            pltpu.VMEM((PAIRS, columns, 2 * rows), bf16),
            pltpu.VMEM((CHUNKS, columns, rows), bf16),
            pltpu.VMEM((CHUNKS, big, rows), bf16),
            pltpu.VMEM((CHUNKS, big, rows), bf16),
            pltpu.VMEM((CHUNKS, big, rows), bf16),
            pltpu.VMEM((PAIRS, big, 2 * rows), bf16),
            pltpu.VMEM((PAIRS, 3, big, lanes), bf16),
            pltpu.VMEM((24, 1, 128), f32),
            pltpu.VMEM((columns, hidden), f32),
            pltpu.VMEM((columns, hidden), f32),
            dma((PIECES + 2,)), dma((2, PIECES)), dma((RING, PIECES)), dma((PIECES,)),
            dma((RING, PIECES)), dma((RING, PIECES)),
            dma((PAIRS,)), dma((CHUNKS, 2)), dma((CHUNKS,)), dma((PAIRS,)), dma((PAIRS,)),
            dma((PAIRS, 2)), dma((PAIRS,)),
            dma((24,)), dma((24,)),
        ],
        compiler_params=pltpu.CompilerParams(
            collective_id=0, has_side_effects=True, vmem_limit_bytes=53 * 2**20
        ),
        cost_estimate=pl.CostEstimate(
            flops=32 * block * hidden * columns, bytes_accessed=16 * 2**20, transcendentals=0
        ),
    )(saved_acts, residual, direction)


def finish_kernel(sums_ref, curved_ref, sol_ref, res_ref, dir_ref, *refs):
    outs, here, sems = refs[:3], refs[3:6], refs[6]
    norm_old, along = sums_ref[0:1, 0:1], sums_ref[0:1, 1:2]
    res_curved, curved_sq = sums_ref[0:1, 2:3], sums_ref[0:1, 3:4]
    step_size = norm_old / along
    norm_new = norm_old + step_size * (step_size * curved_sq - 2.0 * res_curved)
    growth = norm_new / norm_old
    blocks = 4
    size = curved_ref.shape[0] // blocks
    copies = []
    for i in range(blocks):
        at = pl.ds(i * size, size)
        direction = dir_ref[at, :]
        new_residual = res_ref[at, :] - step_size * curved_ref[at, :]
        here[0][at, :] = sol_ref[at, :] + step_size * direction
        here[1][at, :] = new_residual
        here[2][at, :] = new_residual + growth * direction
        for o in range(3):
            copy = pltpu.make_async_copy(here[o].at[at], outs[o].at[at], sems.at[o, i])
            copy.start()
            copies.append(copy)
    for copy in copies:
        copy.wait()


def finish(sums, curved, solution, residual, direction):
    vmem = pl.BlockSpec(memory_space=pltpu.VMEM)
    field = jax.ShapeDtypeStruct(curved.shape, jnp.float32)
    return pl.pallas_call(
        finish_kernel,
        out_shape=(field,) * 3,
        in_specs=[vmem] * 5,
        out_specs=(pl.BlockSpec(memory_space=pltpu.HBM),) * 3,
        scratch_shapes=[pltpu.VMEM(curved.shape, jnp.float32)] * 3
        + [pltpu.SemaphoreType.DMA((3, 4))],
        compiler_params=pltpu.CompilerParams(vmem_limit_bytes=40 * 2**20),
    )(sums, curved, solution, residual, direction)


def body(saved_acts, solution, residual, direction):
    solution, residual, direction = solution.T, residual.T, direction.T
    curved, sums = curvature(saved_acts, residual, direction)
    outs = finish(sums, curved, solution, residual, direction)
    return tuple(out.T for out in outs)


def solution(mesh):
    return jax.shard_map(
        body,
        mesh=mesh,
        in_specs=(P("dp", "mp"), P("mp", "dp"), P("mp", "dp"), P("mp", "dp")),
        out_specs=(P("mp", "dp"), P("mp", "dp"), P("mp", "dp")),
        check_vma=False,
    )
```

```python
import jax
import jax.numpy as jnp
from jax import lax
from jax.experimental import pallas as pl
from jax.experimental.pallas import tpu as pltpu
from jax.sharding import PartitionSpec as P

RING = 4
PIECES = 3
CHUNKS = 2 * RING * PIECES
PAIRS = CHUNKS // 2
SENDS = ((3, 0, 0), (4, 1, 1), (7, 1, 0), (6, 2, 1), (9, 2, 0))
LAG = (1, 4, 7, 10, 13, 18, 23)
RESTS = ((6, 4), (10, 6), (14, 0), (18, 1))
STEPS = CHUNKS + sum(rest for _, rest in RESTS) + LAG[-1]
MESH = pl.DeviceIdType.MESH


def chunk_place(k, turn):
    late, last = lax.div(k + 18, 24), lax.div(k + 6, 24)
    mid = late - last
    away = mid * (2 + turn * (1 - 2 * (lax.rem(lax.div(lax.rem(k + 3, 4), 2), 2)))) + last * 2
    other = (1 - late) * lax.div(k, 3) + (mid + last) * lax.rem(k, 2)
    piece = (1 - late) * lax.rem(k, 3) + mid * (lax.div(k + 2, 4) - 2)
    piece += last * (lax.div(k, 2) - 9)
    return away, other, piece


def kernel(
    acts_ref, res_ref, dir_ref, curved_ref, sums_ref,
    acts, low, tan, part, pass1, got1a, got1b, quad, got2, tiles, dir_here, res_here,
    own_sem, y_send, y_recv, fwd_send, sib_send, sib_recv,
    sent, r1_recv, f1_recv, r2_recv, g1_recv, g2_recv, f2_recv,
    sum_send, sum_recv,
):
    dp, mp = lax.axis_index("dp"), lax.axis_index("mp")
    y, c = dp // 2, dp % 2
    z, x = mp // RING, mp % RING
    block = acts_ref.shape[0]
    rows = block // PIECES
    cols = low.shape[0]
    big = cols // RING
    lanes = 2 * rows // RING
    tokens = acts.shape[0]
    p1 = x * (1 - c) + z * c
    p2 = z * (1 - c) + x * c
    turn = 1 - 2 * c

    def along_y(d):
        return (((y + d + RING) % RING) * 2 + c, mp)

    def plane(to_x, to_z):
        return lax.rem(z + to_z + RING, RING) * RING + lax.rem(x + to_x + RING, RING)

    up, down = plane(1 - c, c), plane(c - 1, -c)
    second = [plane(o * c, o * (1 - c)) for o in range(RING)]
    up_slot, down_slot, far_slot = (lax.rem(p1 + o, RING) for o in (1, 3, 2))
    second_slot = [lax.rem(p2 + o, RING) for o in range(RING)]

    def ahead(k):
        return up + (down - up) * lax.rem(k, 2)

    def behind(k):
        return down + (up - down) * lax.rem(k, 2)

    def ahead_slot(k):
        return up_slot + (down_slot - up_slot) * lax.rem(k, 2)

    def behind_slot(k):
        return down_slot + (up_slot - down_slot) * lax.rem(k, 2)

    sibling = (y * 2 + 1 - c, mp)

    def act_rows(away, other, piece):
        who = lax.rem(y + away, RING) * 2 + lax.rem(c + other, 2)
        return pl.ds(pl.multiple_of(who * block + piece * rows, rows), rows)

    def remote(src, dst, send, recv, to):
        return pltpu.make_async_remote_copy(
            src_ref=src, dst_ref=dst, send_sem=send, recv_sem=recv,
            device_id=to, device_id_type=MESH,
        )

    def own_copy(j):
        return pltpu.make_async_copy(
            acts_ref.at[pl.ds(j * rows, rows)], acts.at[act_rows(0, 0, j)], own_sem.at[j]
        )

    load_dir = pltpu.make_async_copy(dir_ref, dir_here, own_sem.at[PIECES])
    load_res = pltpu.make_async_copy(res_ref, res_here, own_sem.at[PIECES + 1])
    load_dir.start()
    for j in range(PIECES):
        own_copy(j).start()
    load_res.start()
    barrier = pltpu.get_barrier_semaphore()

    @pl.loop(1, 16)
    def _(o):
        pl.semaphore_signal(barrier, inc=1, device_id=(dp, (mp + o) % 16), device_id_type=MESH)

    @pl.loop(1, 8)
    def _(o):
        pl.semaphore_signal(barrier, inc=1, device_id=((dp + o) % 8, mp), device_id_type=MESH)

    load_dir.wait()
    low[...] = dir_here[...].astype(jnp.bfloat16)
    pl.semaphore_wait(barrier, 22)

    def y_copy(j, way):
        here = acts.at[act_rows(0, 0, j)]
        arrives = 1 + 2 * way
        return remote(
            here, here, y_send.at[way, j], y_recv.at[arrives, j], along_y(2 * way - 1)
        )

    def sib_copy(away, j):
        here = acts.at[act_rows(away, 0, j)]
        return remote(here, here, sib_send.at[away, j], sib_recv.at[away, j], sibling)

    def fwd_copy(j):
        here = acts.at[act_rows((RING - turn) % RING, 0, j)]
        return remote(here, here, fwd_send.at[j], y_recv.at[2, j], along_y(turn))

    for j in range(PIECES):
        own_copy(j).wait()
        if j == 0:
            y_copy(j, 1 - c).start()
        sib_copy(0, j).start()
    curved_ref[...] = jnp.zeros_like(curved_ref)

    def slot_rows(slot):
        return pl.ds(pl.multiple_of(slot * big, 16), big)

    def lane(slot):
        return pl.ds(pl.multiple_of(slot * lanes, lanes), lanes)

    def r1_copy(k, which):
        done = sent.at[lax.div(k, 2)]
        if which == 0:
            src = part.at[k, slot_rows(far_slot)]
            return remote(src, pass1.at[k], done, r1_recv.at[k, 0], (dp, ahead(k)))
        src = part.at[k, slot_rows(behind_slot(k))]
        return remote(src, got1b.at[k], done, r1_recv.at[k, 1], (dp, behind(k)))

    def f1_copy(k):
        src = part.at[k, slot_rows(ahead_slot(k))]
        return remote(src, got1a.at[k], sent.at[lax.div(k, 2)], f1_recv.at[k], (dp, ahead(k)))

    def r2_copy(m, o):
        src = quad.at[m, :, lane(second_slot[o])]
        return remote(src, got2.at[m, o - 1], sent.at[m], r2_recv.at[m], (dp, second[o]))

    def g1_copy(m, o):
        here = tan.at[m, slot_rows(p1), lane(p2)]
        return remote(here, here, sent.at[m], g1_recv.at[m], (dp, second[o]))

    def g2_copy(m, way, whose):
        here = tan.at[m, slot_rows(whose)]
        to = behind(m) if way else ahead(m)
        return remote(here, here, sent.at[m], g2_recv.at[m, way], (dp, to))

    def f2_copy(m, whose):
        here = tan.at[m, slot_rows(whose)]
        return remote(here, here, sent.at[m], f2_recv.at[m], (dp, ahead(m)))

    def wait_all(sem, some):
        pltpu.make_async_copy(some, some, sem).wait()

    def arrive(k):
        away, other, piece = chunk_place(k, turn)

        @pl.when((other == 0) & (away != 0))
        def _():
            here = acts.at[act_rows(away, 0, piece)]
            remote(
                here, here, y_send.at[0, 0], y_recv.at[away, piece], sibling
            ).wait_recv()
            sib_copy(away, piece).start()

            @pl.when(away == (RING - turn) % RING)
            def _():
                fwd_copy(piece).start()

        @pl.when(other == 1)
        def _():
            here = acts.at[act_rows(away, 1, piece)]
            remote(
                here, here, sib_send.at[0, 0], sib_recv.at[away, piece], sibling
            ).wait_recv()

    def forward_product(k):
        product = lax.dot_general(
            low[...], acts[act_rows(*chunk_place(k, turn)), :], (((1,), (1,)), ((), ())),
            preferred_element_type=jnp.float32,
        )
        part[k] = product.astype(jnp.bfloat16)
        r1_copy(k, 0).start()
        r1_copy(k, 1).start()

    def pass_on(k):
        r1_copy(k, 0).wait_recv()
        here = slot_rows(ahead_slot(k))
        part[k, here, :] = (
            part[k, here, :].astype(jnp.float32) + pass1[k].astype(jnp.float32)
        ).astype(jnp.bfloat16)
        f1_copy(k).start()

    def quarter(k):
        f1_copy(k).wait_recv()
        r1_copy(k, 1).wait_recv()
        m, odd = lax.div(k, 2), lax.rem(k, 2)
        half = pl.ds(pl.multiple_of(odd * rows, rows), rows)
        quad[m, :, half] = (
            part[k, slot_rows(p1), :].astype(jnp.float32)
            + got1a[k].astype(jnp.float32)
            + got1b[k].astype(jnp.float32)
        ).astype(jnp.bfloat16)

        @pl.when(odd == 1)
        def _():
            for o in range(1, RING):
                r2_copy(m, o).start()

    def total(m):
        wait_all(r2_recv.at[m], got2.at[m])
        value = quad[m, :, lane(p2)].astype(jnp.float32)
        for o in range(1, RING):
            value = value + got2[m, o - 1].astype(jnp.float32)
        tan[m, slot_rows(p1), lane(p2)] = value.astype(jnp.bfloat16)
        for o in range(1, RING):
            g1_copy(m, o).start()

    def spread(m):
        wait_all(g1_recv.at[m], got2.at[m])
        g2_copy(m, 0, p1).start()
        g2_copy(m, 1, p1).start()

    def spread_on(m):
        whose = behind_slot(m)
        g2_copy(m, 0, whose).wait_recv()
        f2_copy(m, whose).start()

    def back_product(m):
        g2_copy(m, 1, ahead_slot(m)).wait_recv()
        f2_copy(m, far_slot).wait_recv()

        @pl.loop(0, acts.shape[1] // WIDE)
        def _(h):
            at = pl.ds(pl.multiple_of(h * WIDE, WIDE), WIDE)
            curved_ref[:, at] += jnp.dot(
                tan[m, :, 0:rows], acts[act_rows(*chunk_place(2 * m, turn)), at],
                preferred_element_type=jnp.float32,
            ) + jnp.dot(
                tan[m, :, rows : 2 * rows], acts[act_rows(*chunk_place(2 * m + 1, turn)), at],
                preferred_element_type=jnp.float32,
            )

        wait_all(sent.at[m], part.at[2 * m])
        wait_all(sent.at[m], part.at[2 * m, pl.ds(0, 2 * big)])
        wait_all(sent.at[m], got2.at[m])
        wait_all(sent.at[m], got2.at[m])
        wait_all(sent.at[m], tan.at[m, pl.ds(0, 3 * big)])

    stages = [
        (LAG[1], pass_on, 1), (LAG[2], quarter, 1), (LAG[3], total, 2), (LAG[4], spread, 2),
        (LAG[5], spread_on, 2), (LAG[0], arrive, 1), (LAG[0], forward_product, 1),
        (LAG[6], back_product, 2),
    ]

    @pl.loop(0, STEPS)
    def _(step):
        for at, j, way in SENDS:

            @pl.when(step == at)
            def _(j=j, way=way):
                y_copy(j, (way + c) % 2).start()

        for lag, stage, every in stages:
            turn_of = step - lag
            k, go, begin = turn_of, turn_of >= 0, 0
            for at, rest in RESTS:
                go &= (turn_of < at + begin) | (turn_of >= at + begin + rest)
                begin += rest
                k = jnp.where(turn_of >= at + begin, turn_of - begin, k)
            go &= turn_of < CHUNKS + begin
            if every == 2:
                go &= lax.rem(k, 2) == 1

            @pl.when(go)
            def _(k=k, stage=stage, every=every):
                stage(lax.div(k, every))

    for j in range(PIECES):
        y_copy(j, 0).wait_send()
        y_copy(j, 1).wait_send()
        fwd_copy(j).wait_send()
        for away in range(RING):
            sib_copy(away, j).wait_send()

    load_res.wait()
    direction, residual = dir_here[...], res_here[...]
    curved = curved_ref[...] / tokens + 1.0 * direction
    curved_ref[...] = curved

    def total_of(v):
        return jnp.sum(jnp.sum(v, axis=0, keepdims=True), axis=1, keepdims=True)

    place = lax.broadcasted_iota(jnp.int32, (1, 128), 1)
    mine = jnp.zeros((1, 128), jnp.float32)
    for i, (a, b) in enumerate(
        ((residual, residual), (direction, curved), (residual, curved), (curved, curved))
    ):
        mine = jnp.where(place == i, total_of(a * b), mine)
    tiles[mp] = mine

    def plane_copy(o, whose):
        here = tiles.at[whose]
        return remote(here, here, sum_send.at[o], sum_recv.at[o], (dp, (mp + o) % 16))

    def column_copy(o, whose):
        here = tiles.at[16 + whose]
        return remote(here, here, sum_send.at[16 + o], sum_recv.at[16 + o], ((dp + o) % 8, mp))

    @pl.loop(1, 16)
    def _(o):
        plane_copy(o, mp).start()

    @pl.loop(1, 16)
    def _(o):
        plane_copy(o, (mp + 16 - o) % 16).wait_recv()

    subtotal = tiles[0]
    for i in range(1, 16):
        subtotal = subtotal + tiles[i]
    tiles[16 + dp] = subtotal

    @pl.loop(1, 8)
    def _(o):
        column_copy(o, dp).start()

    @pl.loop(1, 8)
    def _(o):
        column_copy(o, (dp + 8 - o) % 8).wait_recv()

    whole = tiles[16]
    for i in range(1, 8):
        whole = whole + tiles[16 + i]
    sums_ref[...] = jnp.broadcast_to(whole, (8, 128))

    @pl.loop(1, 16)
    def _(o):
        plane_copy(o, mp).wait_send()

    @pl.loop(1, 8)
    def _(o):
        column_copy(o, dp).wait_send()


WIDE = 384


def curvature(saved_acts, residual, direction):
    block, hidden = saved_acts.shape
    columns = direction.shape[0]
    rows = block // PIECES
    big, lanes = columns // RING, 2 * rows // RING
    bf16, f32 = jnp.bfloat16, jnp.float32
    dma = pltpu.SemaphoreType.DMA
    vmem = pl.BlockSpec(memory_space=pltpu.VMEM)
    return pl.pallas_call(
        kernel,
        out_shape=(
            jax.ShapeDtypeStruct((columns, hidden), f32),
            jax.ShapeDtypeStruct((8, 128), f32),
        ),
        in_specs=[pl.BlockSpec(memory_space=pltpu.HBM)] * 3,
        out_specs=(vmem, vmem),
        scratch_shapes=[
            pltpu.VMEM((8 * block, hidden), bf16),
            pltpu.VMEM((columns, hidden), bf16),
            pltpu.VMEM((PAIRS, columns, 2 * rows), bf16),
            pltpu.VMEM((CHUNKS, columns, rows), bf16),
            pltpu.VMEM((CHUNKS, big, rows), bf16),
            pltpu.VMEM((CHUNKS, big, rows), bf16),
            pltpu.VMEM((CHUNKS, big, rows), bf16),
            pltpu.VMEM((PAIRS, big, 2 * rows), bf16),
            pltpu.VMEM((PAIRS, 3, big, lanes), bf16),
            pltpu.VMEM((24, 1, 128), f32),
            pltpu.VMEM((columns, hidden), f32),
            pltpu.VMEM((columns, hidden), f32),
            dma((PIECES + 2,)), dma((2, PIECES)), dma((RING, PIECES)), dma((PIECES,)),
            dma((RING, PIECES)), dma((RING, PIECES)),
            dma((PAIRS,)), dma((CHUNKS, 2)), dma((CHUNKS,)), dma((PAIRS,)), dma((PAIRS,)),
            dma((PAIRS, 2)), dma((PAIRS,)),
            dma((24,)), dma((24,)),
        ],
        compiler_params=pltpu.CompilerParams(
            collective_id=0, has_side_effects=True, vmem_limit_bytes=53 * 2**20
        ),
        cost_estimate=pl.CostEstimate(
            flops=32 * block * hidden * columns, bytes_accessed=16 * 2**20, transcendentals=0
        ),
    )(saved_acts, residual, direction)


def finish_kernel(sums_ref, curved_ref, sol_ref, res_ref, dir_ref, *refs):
    outs, here, sems = refs[:3], refs[3:6], refs[6]
    norm_old, along = sums_ref[0:1, 0:1], sums_ref[0:1, 1:2]
    res_curved, curved_sq = sums_ref[0:1, 2:3], sums_ref[0:1, 3:4]
    step_size = norm_old / along
    norm_new = norm_old + step_size * (step_size * curved_sq - 2.0 * res_curved)
    growth = norm_new / norm_old
    blocks = 4
    size = curved_ref.shape[0] // blocks
    copies = []
    for i in range(blocks):
        at = pl.ds(i * size, size)
        direction = dir_ref[at, :]
        new_residual = res_ref[at, :] - step_size * curved_ref[at, :]
        here[0][at, :] = sol_ref[at, :] + step_size * direction
        here[1][at, :] = new_residual
        here[2][at, :] = new_residual + growth * direction
        for o in range(3):
            copy = pltpu.make_async_copy(here[o].at[at], outs[o].at[at], sems.at[o, i])
            copy.start()
            copies.append(copy)
    for copy in copies:
        copy.wait()


def finish(sums, curved, solution, residual, direction):
    vmem = pl.BlockSpec(memory_space=pltpu.VMEM)
    field = jax.ShapeDtypeStruct(curved.shape, jnp.float32)
    return pl.pallas_call(
        finish_kernel,
        out_shape=(field,) * 3,
        in_specs=[vmem] * 5,
        out_specs=(pl.BlockSpec(memory_space=pltpu.HBM),) * 3,
        scratch_shapes=[pltpu.VMEM(curved.shape, jnp.float32)] * 3
        + [pltpu.SemaphoreType.DMA((3, 4))],
        compiler_params=pltpu.CompilerParams(vmem_limit_bytes=40 * 2**20),
    )(sums, curved, solution, residual, direction)


def body(saved_acts, solution, residual, direction):
    solution, residual, direction = solution.T, residual.T, direction.T
    curved, sums = curvature(saved_acts, residual, direction)
    outs = finish(sums, curved, solution, residual, direction)
    return tuple(out.T for out in outs)


def solution(mesh):
    return jax.shard_map(
        body,
        mesh=mesh,
        in_specs=(P("dp", "mp"), P("mp", "dp"), P("mp", "dp"), P("mp", "dp")),
        out_specs=(P("mp", "dp"), P("mp", "dp"), P("mp", "dp")),
        check_vma=False,
    )
```

```python
import jax
import jax.numpy as jnp
from jax import lax
from jax.experimental import pallas as pl
from jax.experimental.pallas import tpu as pltpu
from jax.sharding import PartitionSpec as P

RING = 4
PIECES = 3
CHUNKS = 2 * RING * PIECES
PAIRS = CHUNKS // 2
SENDS = ((3, 0, 0), (4, 1, 1), (7, 1, 0), (6, 2, 1), (9, 2, 0))
LAG = (1, 4, 7, 10, 13, 18, 23)
RESTS = ((6, 4), (10, 6), (14, 0), (18, 1))
STEPS = CHUNKS + sum(rest for _, rest in RESTS) + LAG[-1]
MESH = pl.DeviceIdType.MESH


def chunk_place(k, turn):
    late, last = lax.div(k + 18, 24), lax.div(k + 6, 24)
    mid = late - last
    away = mid * (2 + turn * (1 - 2 * (lax.rem(lax.div(lax.rem(k + 3, 4), 2), 2)))) + last * 2
    other = (1 - late) * lax.div(k, 3) + (mid + last) * lax.rem(k, 2)
    piece = (1 - late) * lax.rem(k, 3) + mid * (lax.div(k + 2, 4) - 2)
    piece += last * (lax.div(k, 2) - 9)
    return away, other, piece


def kernel(
    acts_ref, res_ref, dir_ref, curved_ref, sums_ref,
    acts, low, tan, part, pass1, got1a, got1b, quad, got2, tiles, dir_here, res_here,
    own_sem, y_send, y_recv, fwd_send, sib_send, sib_recv,
    sent, r1_recv, f1_recv, r2_recv, g1_recv, g2_recv, f2_recv,
    sum_send, sum_recv,
):
    dp, mp = lax.axis_index("dp"), lax.axis_index("mp")
    y, c = dp // 2, dp % 2
    z, x = mp // RING, mp % RING
    block = acts_ref.shape[0]
    rows = block // PIECES
    cols = low.shape[0]
    big = cols // RING
    lanes = 2 * rows // RING
    tokens = acts.shape[0]
    p1 = x * (1 - c) + z * c
    p2 = z * (1 - c) + x * c
    turn = 1 - 2 * c

    def along_y(d):
        return (((y + d + RING) % RING) * 2 + c, mp)

    def plane(to_x, to_z):
        return lax.rem(z + to_z + RING, RING) * RING + lax.rem(x + to_x + RING, RING)

    up, down = plane(1 - c, c), plane(c - 1, -c)
    second = [plane(o * c, o * (1 - c)) for o in range(RING)]
    up_slot, down_slot, far_slot = (lax.rem(p1 + o, RING) for o in (1, 3, 2))
    second_slot = [lax.rem(p2 + o, RING) for o in range(RING)]

    def ahead(k):
        return up + (down - up) * lax.rem(k, 2)

    def behind(k):
        return down + (up - down) * lax.rem(k, 2)

    def ahead_slot(k):
        return up_slot + (down_slot - up_slot) * lax.rem(k, 2)

    def behind_slot(k):
        return down_slot + (up_slot - down_slot) * lax.rem(k, 2)

    sibling = (y * 2 + 1 - c, mp)

    def act_rows(away, other, piece):
        who = lax.rem(y + away, RING) * 2 + lax.rem(c + other, 2)
        return pl.ds(pl.multiple_of(who * block + piece * rows, rows), rows)

    def remote(src, dst, send, recv, to):
        return pltpu.make_async_remote_copy(
            src_ref=src, dst_ref=dst, send_sem=send, recv_sem=recv,
            device_id=to, device_id_type=MESH,
        )

    def own_copy(j):
        return pltpu.make_async_copy(
            acts_ref.at[pl.ds(j * rows, rows)], acts.at[act_rows(0, 0, j)], own_sem.at[j]
        )

    load_dir = pltpu.make_async_copy(dir_ref, dir_here, own_sem.at[PIECES])
    load_res = pltpu.make_async_copy(res_ref, res_here, own_sem.at[PIECES + 1])
    load_dir.start()
    for j in range(PIECES):
        own_copy(j).start()
    load_res.start()
    barrier = pltpu.get_barrier_semaphore()

    @pl.loop(1, 16)
    def _(o):
        pl.semaphore_signal(barrier, inc=1, device_id=(dp, (mp + o) % 16), device_id_type=MESH)

    @pl.loop(1, 8)
    def _(o):
        pl.semaphore_signal(barrier, inc=1, device_id=((dp + o) % 8, mp), device_id_type=MESH)

    load_dir.wait()
    low[...] = dir_here[...].astype(jnp.bfloat16)
    pl.semaphore_wait(barrier, 22)

    def y_copy(j, way):
        here = acts.at[act_rows(0, 0, j)]
        arrives = 1 + 2 * way
        return remote(
            here, here, y_send.at[way, j], y_recv.at[arrives, j], along_y(2 * way - 1)
        )

    def sib_copy(away, j):
        here = acts.at[act_rows(away, 0, j)]
        return remote(here, here, sib_send.at[away, j], sib_recv.at[away, j], sibling)

    def fwd_copy(j):
        here = acts.at[act_rows((RING - turn) % RING, 0, j)]
        return remote(here, here, fwd_send.at[j], y_recv.at[2, j], along_y(turn))

    for j in range(PIECES):
        own_copy(j).wait()
        if j == 0:
            y_copy(j, 1 - c).start()
        sib_copy(0, j).start()
    curved_ref[...] = jnp.zeros_like(curved_ref)

    def slot_rows(slot):
        return pl.ds(pl.multiple_of(slot * big, 16), big)

    def lane(slot):
        return pl.ds(pl.multiple_of(slot * lanes, lanes), lanes)

    def r1_copy(k, which):
        done = sent.at[lax.div(k, 2)]
        if which == 0:
            src = part.at[k, slot_rows(far_slot)]
            return remote(src, pass1.at[k], done, r1_recv.at[k], (dp, ahead(k)))
        src = part.at[k, slot_rows(behind_slot(k))]
        return remote(src, got1b.at[k], done, f1_recv.at[k], (dp, behind(k)))

    def f1_copy(k):
        src = part.at[k, slot_rows(ahead_slot(k))]
        return remote(src, got1a.at[k], sent.at[lax.div(k, 2)], f1_recv.at[k], (dp, ahead(k)))

    def r2_copy(m, o):
        src = quad.at[m, :, lane(second_slot[o])]
        return remote(src, got2.at[m, o - 1], sent.at[m], r2_recv.at[m], (dp, second[o]))

    def g1_copy(m, o):
        here = tan.at[m, slot_rows(p1), lane(p2)]
        return remote(here, here, sent.at[m], g1_recv.at[m], (dp, second[o]))

    def g2_copy(m, way, whose):
        here = tan.at[m, slot_rows(whose)]
        to = behind(m) if way else ahead(m)
        came = f2_recv.at[m] if way else g2_recv.at[m]
        return remote(here, here, sent.at[m], came, (dp, to))

    def f2_copy(m, whose):
        here = tan.at[m, slot_rows(whose)]
        return remote(here, here, sent.at[m], f2_recv.at[m], (dp, ahead(m)))

    def wait_all(sem, some):
        pltpu.make_async_copy(some, some, sem).wait()

    def arrive(k):
        away, other, piece = chunk_place(k, turn)

        @pl.when((other == 0) & (away != 0))
        def _():
            here = acts.at[act_rows(away, 0, piece)]
            remote(
                here, here, y_send.at[0, 0], y_recv.at[away, piece], sibling
            ).wait_recv()
            sib_copy(away, piece).start()

            @pl.when(away == (RING - turn) % RING)
            def _():
                fwd_copy(piece).start()

        @pl.when(other == 1)
        def _():
            here = acts.at[act_rows(away, 1, piece)]
            remote(
                here, here, sib_send.at[0, 0], sib_recv.at[away, piece], sibling
            ).wait_recv()

    def forward_product(k):
        product = lax.dot_general(
            low[...], acts[act_rows(*chunk_place(k, turn)), :], (((1,), (1,)), ((), ())),
            preferred_element_type=jnp.float32,
        )
        part[k] = product.astype(jnp.bfloat16)
        r1_copy(k, 0).start()
        r1_copy(k, 1).start()

    def pass_on(k):
        r1_copy(k, 0).wait_recv()
        here = slot_rows(ahead_slot(k))
        part[k, here, :] = (
            part[k, here, :].astype(jnp.float32) + pass1[k].astype(jnp.float32)
        ).astype(jnp.bfloat16)
        f1_copy(k).start()

    def quarter(k):
        wait_all(f1_recv.at[k], part.at[k, pl.ds(0, 2 * big)])
        m, odd = lax.div(k, 2), lax.rem(k, 2)
        half = pl.ds(pl.multiple_of(odd * rows, rows), rows)
        quad[m, :, half] = (
            part[k, slot_rows(p1), :].astype(jnp.float32)
            + got1a[k].astype(jnp.float32)
            + got1b[k].astype(jnp.float32)
        ).astype(jnp.bfloat16)

        @pl.when(odd == 1)
        def _():
            for o in range(1, RING):
                r2_copy(m, o).start()

    def total(m):
        wait_all(r2_recv.at[m], got2.at[m])
        value = quad[m, :, lane(p2)].astype(jnp.float32)
        for o in range(1, RING):
            value = value + got2[m, o - 1].astype(jnp.float32)
        tan[m, slot_rows(p1), lane(p2)] = value.astype(jnp.bfloat16)
        for o in range(1, RING):
            g1_copy(m, o).start()

    def spread(m):
        wait_all(g1_recv.at[m], got2.at[m])
        g2_copy(m, 0, p1).start()
        g2_copy(m, 1, p1).start()

    def spread_on(m):
        whose = behind_slot(m)
        g2_copy(m, 0, whose).wait_recv()
        f2_copy(m, whose).start()

    def back_product(m):
        wait_all(f2_recv.at[m], tan.at[m, pl.ds(0, 2 * big)])

        @pl.loop(0, acts.shape[1] // WIDE)
        def _(h):
            at = pl.ds(pl.multiple_of(h * WIDE, WIDE), WIDE)
            curved_ref[:, at] += jnp.dot(
                tan[m, :, 0:rows], acts[act_rows(*chunk_place(2 * m, turn)), at],
                preferred_element_type=jnp.float32,
            ) + jnp.dot(
                tan[m, :, rows : 2 * rows], acts[act_rows(*chunk_place(2 * m + 1, turn)), at],
                preferred_element_type=jnp.float32,
            )

        wait_all(sent.at[m], part.at[2 * m])
        wait_all(sent.at[m], part.at[2 * m, pl.ds(0, 2 * big)])
        wait_all(sent.at[m], got2.at[m])
        wait_all(sent.at[m], got2.at[m])
        wait_all(sent.at[m], tan.at[m, pl.ds(0, 3 * big)])

    stages = [
        (LAG[1], pass_on, 1), (LAG[2], quarter, 1), (LAG[3], total, 2), (LAG[4], spread, 2),
        (LAG[5], spread_on, 2), (LAG[0], arrive, 1), (LAG[0], forward_product, 1),
        (LAG[6], back_product, 2),
    ]

    @pl.loop(0, STEPS)
    def _(step):
        for at, j, way in SENDS:

            @pl.when(step == at)
            def _(j=j, way=way):
                y_copy(j, (way + c) % 2).start()

        for lag, stage, every in stages:
            turn_of = step - lag
            k, go, begin = turn_of, turn_of >= 0, 0
            for at, rest in RESTS:
                go &= (turn_of < at + begin) | (turn_of >= at + begin + rest)
                begin += rest
                k = jnp.where(turn_of >= at + begin, turn_of - begin, k)
            go &= turn_of < CHUNKS + begin
            if every == 2:
                go &= lax.rem(k, 2) == 1

            @pl.when(go)
            def _(k=k, stage=stage, every=every):
                stage(lax.div(k, every))

    load_res.wait()
    direction, residual = dir_here[...], res_here[...]
    curved = curved_ref[...] / tokens + 1.0 * direction
    curved_ref[...] = curved

    def total_of(v):
        return jnp.sum(jnp.sum(v, axis=0, keepdims=True), axis=1, keepdims=True)

    place = lax.broadcasted_iota(jnp.int32, (1, 128), 1)
    mine = jnp.zeros((1, 128), jnp.float32)
    for i, (a, b) in enumerate(
        ((residual, residual), (direction, curved), (residual, curved), (curved, curved))
    ):
        mine = jnp.where(place == i, total_of(a * b), mine)
    tiles[mp] = mine

    def plane_copy(o, whose):
        here = tiles.at[whose]
        return remote(here, here, sum_send.at[0], sum_recv.at[0], (dp, (mp + o) % 16))

    def column_copy(o, whose):
        here = tiles.at[16 + whose]
        return remote(here, here, sum_send.at[1], sum_recv.at[1], ((dp + o) % 8, mp))

    @pl.loop(1, 16)
    def _(o):
        plane_copy(o, mp).start()

    for j in range(PIECES):
        y_copy(j, 0).wait_send()
        y_copy(j, 1).wait_send()
        fwd_copy(j).wait_send()
        for away in range(RING):
            sib_copy(away, j).wait_send()

    wait_all(sum_recv.at[0], tiles.at[pl.ds(0, 15)])

    subtotal = tiles[0]
    for i in range(1, 16):
        subtotal = subtotal + tiles[i]
    tiles[16 + dp] = subtotal

    @pl.loop(1, 8)
    def _(o):
        column_copy(o, dp).start()

    wait_all(sum_recv.at[1], tiles.at[pl.ds(0, 7)])

    whole = tiles[16]
    for i in range(1, 8):
        whole = whole + tiles[16 + i]
    sums_ref[...] = jnp.broadcast_to(whole, (8, 128))

    wait_all(sum_send.at[0], tiles.at[pl.ds(0, 15)])
    wait_all(sum_send.at[1], tiles.at[pl.ds(0, 7)])


WIDE = 384


def curvature(saved_acts, residual, direction):
    block, hidden = saved_acts.shape
    columns = direction.shape[0]
    rows = block // PIECES
    big, lanes = columns // RING, 2 * rows // RING
    bf16, f32 = jnp.bfloat16, jnp.float32
    dma = pltpu.SemaphoreType.DMA
    vmem = pl.BlockSpec(memory_space=pltpu.VMEM)
    return pl.pallas_call(
        kernel,
        out_shape=(
            jax.ShapeDtypeStruct((columns, hidden), f32),
            jax.ShapeDtypeStruct((8, 128), f32),
        ),
        in_specs=[pl.BlockSpec(memory_space=pltpu.HBM)] * 3,
        out_specs=(vmem, vmem),
        scratch_shapes=[
            pltpu.VMEM((8 * block, hidden), bf16),
            pltpu.VMEM((columns, hidden), bf16),
            pltpu.VMEM((PAIRS, columns, 2 * rows), bf16),
            pltpu.VMEM((CHUNKS, columns, rows), bf16),
            pltpu.VMEM((CHUNKS, big, rows), bf16),
            pltpu.VMEM((CHUNKS, big, rows), bf16),
            pltpu.VMEM((CHUNKS, big, rows), bf16),
            pltpu.VMEM((PAIRS, big, 2 * rows), bf16),
            pltpu.VMEM((PAIRS, 3, big, lanes), bf16),
            pltpu.VMEM((24, 1, 128), f32),
            pltpu.VMEM((columns, hidden), f32),
            pltpu.VMEM((columns, hidden), f32),
            dma((PIECES + 2,)), dma((2, PIECES)), dma((RING, PIECES)), dma((PIECES,)),
            dma((RING, PIECES)), dma((RING, PIECES)),
            dma((PAIRS,)), dma((CHUNKS,)), dma((CHUNKS,)), dma((PAIRS,)), dma((PAIRS,)),
            dma((PAIRS,)), dma((PAIRS,)),
            dma((2,)), dma((2,)),
        ],
        compiler_params=pltpu.CompilerParams(
            collective_id=0, has_side_effects=True, vmem_limit_bytes=53 * 2**20
        ),
        cost_estimate=pl.CostEstimate(
            flops=32 * block * hidden * columns, bytes_accessed=16 * 2**20, transcendentals=0
        ),
    )(saved_acts, residual, direction)


def finish_kernel(sums_ref, curved_ref, sol_ref, res_ref, dir_ref, *refs):
    outs, here, sems = refs[:3], refs[3:6], refs[6]
    norm_old, along = sums_ref[0:1, 0:1], sums_ref[0:1, 1:2]
    res_curved, curved_sq = sums_ref[0:1, 2:3], sums_ref[0:1, 3:4]
    step_size = norm_old / along
    norm_new = norm_old + step_size * (step_size * curved_sq - 2.0 * res_curved)
    growth = norm_new / norm_old
    blocks = 4
    size = curved_ref.shape[0] // blocks
    copies = []
    for i in range(blocks):
        at = pl.ds(i * size, size)
        direction = dir_ref[at, :]
        new_residual = res_ref[at, :] - step_size * curved_ref[at, :]
        here[0][at, :] = sol_ref[at, :] + step_size * direction
        here[1][at, :] = new_residual
        here[2][at, :] = new_residual + growth * direction
        for o in range(3):
            copy = pltpu.make_async_copy(here[o].at[at], outs[o].at[at], sems.at[o, i])
            copy.start()
            copies.append(copy)
    for copy in copies:
        copy.wait()


def finish(sums, curved, solution, residual, direction):
    vmem = pl.BlockSpec(memory_space=pltpu.VMEM)
    field = jax.ShapeDtypeStruct(curved.shape, jnp.float32)
    return pl.pallas_call(
        finish_kernel,
        out_shape=(field,) * 3,
        in_specs=[vmem] * 5,
        out_specs=(pl.BlockSpec(memory_space=pltpu.HBM),) * 3,
        scratch_shapes=[pltpu.VMEM(curved.shape, jnp.float32)] * 3
        + [pltpu.SemaphoreType.DMA((3, 4))],
        compiler_params=pltpu.CompilerParams(vmem_limit_bytes=40 * 2**20),
    )(sums, curved, solution, residual, direction)


def body(saved_acts, solution, residual, direction):
    solution, residual, direction = solution.T, residual.T, direction.T
    curved, sums = curvature(saved_acts, residual, direction)
    outs = finish(sums, curved, solution, residual, direction)
    return tuple(out.T for out in outs)


def solution(mesh):
    return jax.shard_map(
        body,
        mesh=mesh,
        in_specs=(P("dp", "mp"), P("mp", "dp"), P("mp", "dp"), P("mp", "dp")),
        out_specs=(P("mp", "dp"), P("mp", "dp"), P("mp", "dp")),
        check_vma=False,
    )
```

```python
import jax
import jax.numpy as jnp
from jax import lax
from jax.experimental import pallas as pl
from jax.experimental.pallas import tpu as pltpu
from jax.sharding import PartitionSpec as P

RING = 4
PIECES = 3
CHUNKS = 2 * RING * PIECES
PAIRS = CHUNKS // 2
SENDS = ((3, 0, 0), (4, 1, 1), (7, 1, 0), (6, 2, 1), (9, 2, 0))
LAG = (1, 4, 7, 9, 12, 17, 22)
RESTS = ((6, 4), (10, 6))
STEPS = CHUNKS + sum(rest for _, rest in RESTS) + LAG[-1]
MESH = pl.DeviceIdType.MESH


def chunk_place(k, turn):
    late, last = lax.div(k + 18, 24), lax.div(k + 6, 24)
    mid = late - last
    away = mid * (2 + turn * (1 - 2 * (lax.rem(lax.div(lax.rem(k + 3, 4), 2), 2)))) + last * 2
    other = (1 - late) * lax.div(k, 3) + (mid + last) * lax.rem(k, 2)
    piece = (1 - late) * lax.rem(k, 3) + mid * (lax.div(k + 2, 4) - 2)
    piece += last * (lax.div(k, 2) - 9)
    return away, other, piece


def kernel(
    acts_ref, res_ref, dir_ref, curved_ref, sums_ref,
    acts, low, tan, part, pass1, got1a, got1b, quad, got2, tiles, dir_here, res_here,
    own_sem, y_send, y_recv, fwd_send, sib_send, sib_recv,
    sent, r1_recv, f1_recv, r2_recv, g1_recv, g2_recv, f2_recv,
    sum_send, sum_recv,
):
    dp, mp = lax.axis_index("dp"), lax.axis_index("mp")
    y, c = dp // 2, dp % 2
    z, x = mp // RING, mp % RING
    block = acts_ref.shape[0]
    rows = block // PIECES
    cols = low.shape[0]
    big = cols // RING
    lanes = 2 * rows // RING
    tokens = acts.shape[0]
    p1 = x * (1 - c) + z * c
    p2 = z * (1 - c) + x * c
    turn = 1 - 2 * c

    def along_y(d):
        return (((y + d + RING) % RING) * 2 + c, mp)

    def plane(to_x, to_z):
        return lax.rem(z + to_z + RING, RING) * RING + lax.rem(x + to_x + RING, RING)

    up, down = plane(1 - c, c), plane(c - 1, -c)
    second = [plane(o * c, o * (1 - c)) for o in range(RING)]
    up_slot, down_slot, far_slot = (lax.rem(p1 + o, RING) for o in (1, 3, 2))
    second_slot = [lax.rem(p2 + o, RING) for o in range(RING)]

    def ahead(k):
        return up + (down - up) * lax.rem(k, 2)

    def behind(k):
        return down + (up - down) * lax.rem(k, 2)

    def ahead_slot(k):
        return up_slot + (down_slot - up_slot) * lax.rem(k, 2)

    def behind_slot(k):
        return down_slot + (up_slot - down_slot) * lax.rem(k, 2)

    sibling = (y * 2 + 1 - c, mp)

    def act_rows(away, other, piece):
        who = lax.rem(y + away, RING) * 2 + lax.rem(c + other, 2)
        return pl.ds(pl.multiple_of(who * block + piece * rows, rows), rows)

    def remote(src, dst, send, recv, to):
        return pltpu.make_async_remote_copy(
            src_ref=src, dst_ref=dst, send_sem=send, recv_sem=recv,
            device_id=to, device_id_type=MESH,
        )

    def own_copy(j):
        return pltpu.make_async_copy(
            acts_ref.at[pl.ds(j * rows, rows)], acts.at[act_rows(0, 0, j)], own_sem.at[j]
        )

    load_dir = pltpu.make_async_copy(dir_ref, dir_here, own_sem.at[PIECES])
    load_res = pltpu.make_async_copy(res_ref, res_here, own_sem.at[PIECES + 1])
    load_dir.start()
    for j in range(PIECES):
        own_copy(j).start()
    load_res.start()
    barrier = pltpu.get_barrier_semaphore()

    @pl.loop(1, 16)
    def _(o):
        pl.semaphore_signal(barrier, inc=1, device_id=(dp, (mp + o) % 16), device_id_type=MESH)

    @pl.loop(1, 8)
    def _(o):
        pl.semaphore_signal(barrier, inc=1, device_id=((dp + o) % 8, mp), device_id_type=MESH)

    load_dir.wait()
    low[...] = dir_here[...].astype(jnp.bfloat16)
    pl.semaphore_wait(barrier, 22)

    def y_copy(j, way):
        here = acts.at[act_rows(0, 0, j)]
        arrives = 1 + 2 * way
        return remote(
            here, here, y_send.at[way, j], y_recv.at[arrives, j], along_y(2 * way - 1)
        )

    def sib_copy(away, j):
        here = acts.at[act_rows(away, 0, j)]
        return remote(here, here, sib_send.at[away, j], sib_recv.at[away, j], sibling)

    def fwd_copy(j):
        here = acts.at[act_rows((RING - turn) % RING, 0, j)]
        return remote(here, here, fwd_send.at[j], y_recv.at[2, j], along_y(turn))

    for j in range(PIECES):
        own_copy(j).wait()
        if j == 0:
            y_copy(j, 1 - c).start()
        sib_copy(0, j).start()
    curved_ref[...] = jnp.zeros_like(curved_ref)

    def slot_rows(slot):
        return pl.ds(pl.multiple_of(slot * big, 16), big)

    def lane(slot):
        return pl.ds(pl.multiple_of(slot * lanes, lanes), lanes)

    def r1_copy(k, which):
        done = sent.at[lax.div(k, 2)]
        if which == 0:
            src = part.at[k, slot_rows(far_slot)]
            return remote(src, pass1.at[k], done, r1_recv.at[k], (dp, ahead(k)))
        src = part.at[k, slot_rows(behind_slot(k))]
        return remote(src, got1b.at[k], done, f1_recv.at[k], (dp, behind(k)))

    def f1_copy(k):
        src = part.at[k, slot_rows(ahead_slot(k))]
        return remote(src, got1a.at[k], sent.at[lax.div(k, 2)], f1_recv.at[k], (dp, ahead(k)))

    def r2_copy(m, o):
        src = quad.at[m, :, lane(second_slot[o])]
        return remote(src, got2.at[m, o - 1], sent.at[m], r2_recv.at[m], (dp, second[o]))

    def g1_copy(m, o):
        here = tan.at[m, slot_rows(p1), lane(p2)]
        return remote(here, here, sent.at[m], g1_recv.at[m], (dp, second[o]))

    def g2_copy(m, way, whose):
        here = tan.at[m, slot_rows(whose)]
        to = behind(m) if way else ahead(m)
        came = f2_recv.at[m] if way else g2_recv.at[m]
        return remote(here, here, sent.at[m], came, (dp, to))

    def f2_copy(m, whose):
        here = tan.at[m, slot_rows(whose)]
        return remote(here, here, sent.at[m], f2_recv.at[m], (dp, ahead(m)))

    def wait_all(sem, some):
        pltpu.make_async_copy(some, some, sem).wait()

    def arrive(k):
        away, other, piece = chunk_place(k, turn)

        @pl.when((other == 0) & (away != 0))
        def _():
            here = acts.at[act_rows(away, 0, piece)]
            remote(
                here, here, y_send.at[0, 0], y_recv.at[away, piece], sibling
            ).wait_recv()
            sib_copy(away, piece).start()

            @pl.when(away == (RING - turn) % RING)
            def _():
                fwd_copy(piece).start()

        @pl.when(other == 1)
        def _():
            here = acts.at[act_rows(away, 1, piece)]
            remote(
                here, here, sib_send.at[0, 0], sib_recv.at[away, piece], sibling
            ).wait_recv()

    def forward_product(k):
        product = lax.dot_general(
            low[...], acts[act_rows(*chunk_place(k, turn)), :], (((1,), (1,)), ((), ())),
            preferred_element_type=jnp.float32,
        )
        part[k] = product.astype(jnp.bfloat16)
        r1_copy(k, 0).start()
        r1_copy(k, 1).start()

    def pass_on(k):
        r1_copy(k, 0).wait_recv()
        here = slot_rows(ahead_slot(k))
        part[k, here, :] = (
            part[k, here, :].astype(jnp.float32) + pass1[k].astype(jnp.float32)
        ).astype(jnp.bfloat16)
        f1_copy(k).start()

    def quarter(k):
        wait_all(f1_recv.at[k], part.at[k, pl.ds(0, 2 * big)])
        m, odd = lax.div(k, 2), lax.rem(k, 2)
        half = pl.ds(pl.multiple_of(odd * rows, rows), rows)
        quad[m, :, half] = (
            part[k, slot_rows(p1), :].astype(jnp.float32)
            + got1a[k].astype(jnp.float32)
            + got1b[k].astype(jnp.float32)
        ).astype(jnp.bfloat16)

        @pl.when(odd == 1)
        def _():
            for o in range(1, RING):
                r2_copy(m, o).start()

    def total(m):
        wait_all(r2_recv.at[m], got2.at[m])
        value = quad[m, :, lane(p2)].astype(jnp.float32)
        for o in range(1, RING):
            value = value + got2[m, o - 1].astype(jnp.float32)
        tan[m, slot_rows(p1), lane(p2)] = value.astype(jnp.bfloat16)
        for o in range(1, RING):
            g1_copy(m, o).start()

    def spread(m):
        wait_all(g1_recv.at[m], got2.at[m])
        g2_copy(m, 0, p1).start()
        g2_copy(m, 1, p1).start()

    def spread_on(m):
        whose = behind_slot(m)
        g2_copy(m, 0, whose).wait_recv()
        f2_copy(m, whose).start()

    def back_product(m):
        wait_all(f2_recv.at[m], tan.at[m, pl.ds(0, 2 * big)])

        @pl.loop(0, acts.shape[1] // WIDE)
        def _(h):
            at = pl.ds(pl.multiple_of(h * WIDE, WIDE), WIDE)
            curved_ref[:, at] += jnp.dot(
                tan[m, :, 0:rows], acts[act_rows(*chunk_place(2 * m, turn)), at],
                preferred_element_type=jnp.float32,
            ) + jnp.dot(
                tan[m, :, rows : 2 * rows], acts[act_rows(*chunk_place(2 * m + 1, turn)), at],
                preferred_element_type=jnp.float32,
            )

        wait_all(sent.at[m], part.at[2 * m])
        wait_all(sent.at[m], part.at[2 * m, pl.ds(0, 2 * big)])
        wait_all(sent.at[m], got2.at[m])
        wait_all(sent.at[m], got2.at[m])
        wait_all(sent.at[m], tan.at[m, pl.ds(0, 3 * big)])

    stages = [
        (LAG[1], pass_on, 1), (LAG[2], quarter, 1), (LAG[3], total, 2), (LAG[4], spread, 2),
        (LAG[5], spread_on, 2), (LAG[0], arrive, 1), (LAG[0], forward_product, 1),
        (LAG[6], back_product, 2),
    ]

    @pl.loop(0, STEPS)
    def _(step):
        for at, j, way in SENDS:

            @pl.when(step == at)
            def _(j=j, way=way):
                y_copy(j, (way + c) % 2).start()

        for lag, stage, every in stages:
            turn_of = step - lag
            k, go, begin = turn_of, turn_of >= 0, 0
            for at, rest in RESTS:
                go &= (turn_of < at + begin) | (turn_of >= at + begin + rest)
                begin += rest
                k = jnp.where(turn_of >= at + begin, turn_of - begin, k)
            go &= turn_of < CHUNKS + begin
            if every == 2:
                go &= lax.rem(k, 2) == 1

            @pl.when(go)
            def _(k=k, stage=stage, every=every):
                stage(lax.div(k, every))

    load_res.wait()
    direction, residual = dir_here[...], res_here[...]
    curved = curved_ref[...] / tokens + 1.0 * direction
    curved_ref[...] = curved

    def total_of(v):
        return jnp.sum(jnp.sum(v, axis=0, keepdims=True), axis=1, keepdims=True)

    place = lax.broadcasted_iota(jnp.int32, (1, 128), 1)
    mine = jnp.zeros((1, 128), jnp.float32)
    for i, (a, b) in enumerate(
        ((residual, residual), (direction, curved), (residual, curved), (curved, curved))
    ):
        mine = jnp.where(place == i, total_of(a * b), mine)
    tiles[mp] = mine

    def plane_copy(o, whose):
        here = tiles.at[whose]
        return remote(here, here, sum_send.at[0], sum_recv.at[0], (dp, (mp + o) % 16))

    def column_copy(o, whose):
        here = tiles.at[16 + whose]
        return remote(here, here, sum_send.at[1], sum_recv.at[1], ((dp + o) % 8, mp))

    @pl.loop(1, 16)
    def _(o):
        plane_copy(o, mp).start()

    for j in range(PIECES):
        y_copy(j, 0).wait_send()
        y_copy(j, 1).wait_send()
        fwd_copy(j).wait_send()
        for away in range(RING):
            sib_copy(away, j).wait_send()

    wait_all(sum_recv.at[0], tiles.at[pl.ds(0, 15)])

    subtotal = tiles[0]
    for i in range(1, 16):
        subtotal = subtotal + tiles[i]
    tiles[16 + dp] = subtotal

    @pl.loop(1, 8)
    def _(o):
        column_copy(o, dp).start()

    wait_all(sum_recv.at[1], tiles.at[pl.ds(0, 7)])

    whole = tiles[16]
    for i in range(1, 8):
        whole = whole + tiles[16 + i]
    sums_ref[...] = jnp.broadcast_to(whole, (8, 128))

    wait_all(sum_send.at[0], tiles.at[pl.ds(0, 15)])
    wait_all(sum_send.at[1], tiles.at[pl.ds(0, 7)])


WIDE = 384


def curvature(saved_acts, residual, direction):
    block, hidden = saved_acts.shape
    columns = direction.shape[0]
    rows = block // PIECES
    big, lanes = columns // RING, 2 * rows // RING
    bf16, f32 = jnp.bfloat16, jnp.float32
    dma = pltpu.SemaphoreType.DMA
    vmem = pl.BlockSpec(memory_space=pltpu.VMEM)
    return pl.pallas_call(
        kernel,
        out_shape=(
            jax.ShapeDtypeStruct((columns, hidden), f32),
            jax.ShapeDtypeStruct((8, 128), f32),
        ),
        in_specs=[pl.BlockSpec(memory_space=pltpu.HBM)] * 3,
        out_specs=(vmem, vmem),
        scratch_shapes=[
            pltpu.VMEM((8 * block, hidden), bf16),
            pltpu.VMEM((columns, hidden), bf16),
            pltpu.VMEM((PAIRS, columns, 2 * rows), bf16),
            pltpu.VMEM((CHUNKS, columns, rows), bf16),
            pltpu.VMEM((CHUNKS, big, rows), bf16),
            pltpu.VMEM((CHUNKS, big, rows), bf16),
            pltpu.VMEM((CHUNKS, big, rows), bf16),
            pltpu.VMEM((PAIRS, big, 2 * rows), bf16),
            pltpu.VMEM((PAIRS, 3, big, lanes), bf16),
            pltpu.VMEM((24, 1, 128), f32),
            pltpu.VMEM((columns, hidden), f32),
            pltpu.VMEM((columns, hidden), f32),
            dma((PIECES + 2,)), dma((2, PIECES)), dma((RING, PIECES)), dma((PIECES,)),
            dma((RING, PIECES)), dma((RING, PIECES)),
            dma((PAIRS,)), dma((CHUNKS,)), dma((CHUNKS,)), dma((PAIRS,)), dma((PAIRS,)),
            dma((PAIRS,)), dma((PAIRS,)),
            dma((2,)), dma((2,)),
        ],
        compiler_params=pltpu.CompilerParams(
            collective_id=0, has_side_effects=True, vmem_limit_bytes=53 * 2**20
        ),
        cost_estimate=pl.CostEstimate(
            flops=32 * block * hidden * columns, bytes_accessed=16 * 2**20, transcendentals=0
        ),
    )(saved_acts, residual, direction)


def finish_kernel(sums_ref, curved_ref, sol_ref, res_ref, dir_ref, *refs):
    outs, here, sems = refs[:3], refs[3:6], refs[6]
    norm_old, along = sums_ref[0:1, 0:1], sums_ref[0:1, 1:2]
    res_curved, curved_sq = sums_ref[0:1, 2:3], sums_ref[0:1, 3:4]
    step_size = norm_old / along
    norm_new = norm_old + step_size * (step_size * curved_sq - 2.0 * res_curved)
    growth = norm_new / norm_old
    blocks = 4
    size = curved_ref.shape[0] // blocks
    copies = []
    for i in range(blocks):
        at = pl.ds(i * size, size)
        direction = dir_ref[at, :]
        new_residual = res_ref[at, :] - step_size * curved_ref[at, :]
        here[0][at, :] = sol_ref[at, :] + step_size * direction
        here[1][at, :] = new_residual
        here[2][at, :] = new_residual + growth * direction
        for o in range(3):
            copy = pltpu.make_async_copy(here[o].at[at], outs[o].at[at], sems.at[o, i])
            copy.start()
            copies.append(copy)
    for copy in copies:
        copy.wait()


def finish(sums, curved, solution, residual, direction):
    vmem = pl.BlockSpec(memory_space=pltpu.VMEM)
    field = jax.ShapeDtypeStruct(curved.shape, jnp.float32)
    return pl.pallas_call(
        finish_kernel,
        out_shape=(field,) * 3,
        in_specs=[vmem] * 5,
        out_specs=(pl.BlockSpec(memory_space=pltpu.HBM),) * 3,
        scratch_shapes=[pltpu.VMEM(curved.shape, jnp.float32)] * 3
        + [pltpu.SemaphoreType.DMA((3, 4))],
        compiler_params=pltpu.CompilerParams(vmem_limit_bytes=40 * 2**20),
    )(sums, curved, solution, residual, direction)


def body(saved_acts, solution, residual, direction):
    solution, residual, direction = solution.T, residual.T, direction.T
    curved, sums = curvature(saved_acts, residual, direction)
    outs = finish(sums, curved, solution, residual, direction)
    return tuple(out.T for out in outs)


def solution(mesh):
    return jax.shard_map(
        body,
        mesh=mesh,
        in_specs=(P("dp", "mp"), P("mp", "dp"), P("mp", "dp"), P("mp", "dp")),
        out_specs=(P("mp", "dp"), P("mp", "dp"), P("mp", "dp")),
        check_vma=False,
    )
```
